128 devices in a mesh: depth: 2 (over core), tile: 64 (over z, y, x).
Axes of the slice: x: 4, y: 4, z: 4, core: 2. Of those that a mesh axis runs over, the one named last changes fastest.
Arguments:
- transmission: bfloat16 [2, 2, 2048, 16384], P('depth', None, None, 'tile')
- chirp_taps: float32 [5], replicated, may hold values from -0.06 to 0.06
- probe_field: float32 [2, 256, 256], replicated, may hold values from -6 to 6
- records: bfloat16 [64, 2, 256, 256], P('tile'), may hold values from 0 to 2
- pos_row: int32 [64, 2], P('tile'), may hold values from 0 to 1792
- pos_col: int32 [64, 2], P('tile'), may hold values from 0 to 255
- counts: int32 [64], P('tile'), may hold values from 1 to 2, as said below
Outputs:
- gradient: bfloat16 [2, 2, 2048, 16384], P('depth', None, None, 'tile')
The draws below stay inside these ranges and needn't reach their ends.
Inputs may be any that keep to these rules, and one draw needn't show every extreme that they name: Slots 0 to counts[t] - 1 of tile t are live; some tile has 2.
All inputs are finite; a program needn't handle non-finite values.
Results may differ from the reference program's by a relative error of at most 0.011.
Values may be sent and summed in bfloat16 or wider, within the bound.
No kernel may reach another device: no remote copies, remote signals or barrier semaphores. Data moves between devices by JAX's collectives and lax.ppermute only.
A program may use at most 64 MiB of HBM per device.

```python
import math
import jax
import jax.numpy as jnp
from jax import lax

W = 256
REACH = 4
SL = 1
TW = 256
H = 2048
CAP = 2
TILES = 64
SLICES = 2
NX = 16384
N_DEPTH = 2


def draw_transmission(key, part):
    first_key, second_key = jax.random.split(key)
    shape_here = (SLICES, H, NX)
    phase = jax.random.uniform(first_key, shape_here, jnp.float32, -math.pi, math.pi)
    amplitude = jnp.exp(jax.random.uniform(second_key, shape_here, jnp.float32, math.log(0.96), 0.0))
    return jnp.stack([amplitude * jnp.cos(phase), amplitude * jnp.sin(phase)], axis=1).astype(jnp.bfloat16)


def draw_counts(key, part):
    first_key, second_key, third_key = jax.random.split(key, 3)
    rolled = jax.random.randint(first_key, (TILES,), 0, 10)
    extra = jax.random.randint(second_key, (TILES,), 1, CAP + 1)
    values = jnp.where(rolled < 3, extra, 1)
    chosen = jax.random.randint(third_key, (), 0, TILES)
    values = jnp.where(jnp.arange(TILES) == chosen, CAP, values)
    return values.astype(jnp.int32)


def set_ends(values, stream_key, low, largest):
    longest = values.shape.index(max(values.shape))
    spots = []
    for shift in (0, 1):
        where = [jax.random.randint(jax.random.fold_in(stream_key, axis), (), 0, length) for axis, length in enumerate(values.shape)]
        where[longest] = (where[longest] + shift) % values.shape[longest]
        spots.append(tuple(where))
    return values.at[spots[0]].set(low).at[spots[1]].set(largest)


def steps_of(key, extent, cuts, least, top_value):
    gain, own = 1.0, jax.random.fold_in(key, 6)
    for position, parts in cuts:
        heights = jnp.exp(jax.random.uniform(jax.random.fold_in(own, position), (parts,), jnp.float32, least / len(cuts), top_value / len(cuts)))
        gain = gain * jnp.repeat(heights, extent[position] // parts).reshape([-1 if axis == position else 1 for axis in range(len(extent))])
    return gain


def gaussian(own_key, dims, deviation, limit, kind=jnp.bfloat16):
    return jnp.clip(deviation * jax.random.normal(own_key, dims, jnp.float32), -limit, limit).astype(kind)


def setup_inputs(seed: int = 0) -> dict:
    splits = jax.random.split(jax.random.key(seed), 8)
    return {
        "transmission": draw_transmission(jax.random.fold_in(splits[7], 71), 0),
        "chirp_taps": jnp.clip(jax.random.uniform(splits[1], (REACH + 1,), jnp.float32, -0.06, 0.06), -0.06, 0.06),
        "probe_field": gaussian(splits[2], (2, W, W), 1.0, 6.0, jnp.float32),
        "records": jnp.clip(2.0 * jax.random.uniform(splits[3], (TILES, CAP, W, W), jnp.float32) ** steps_of(splits[3], (TILES, CAP, W, W), ((0, 64),), -0.2, 0.2), 0.0, 2.0).astype(jnp.bfloat16),
        "pos_row": set_ends(jax.random.randint(splits[4], (TILES, CAP), 0, H - W + 1), jax.random.fold_in(splits[4], 1), 0, H - W).astype(jnp.int32),
        "pos_col": set_ends(jax.random.randint(splits[5], (TILES, CAP), 0, TW), jax.random.fold_in(splits[5], 1), 0, TW - 1).astype(jnp.int32),
        "counts": draw_counts(jax.random.fold_in(splits[7], 71), 0),
    }


def spread_taps(values, chirp_taps, axis_pos):
    reach = chirp_taps.shape[0] - 1
    length = values.shape[axis_pos]
    widths = [(0, 0)] * values.ndim
    widths[axis_pos] = (reach, reach)
    padded = jnp.pad(values, widths)
    total = chirp_taps[0] * values
    for offset in range(1, reach + 1):
        upper = lax.slice_in_dim(padded, reach + offset, reach + offset + length, axis=axis_pos)
        lower = lax.slice_in_dim(padded, reach - offset, reach - offset + length, axis=axis_pos)
        total = total + chirp_taps[offset] * (upper + lower)
    return total

def propagate(wavefield, chirp_taps, sign_value):
    for axis_neg in (-1, -2):
        real_part = wavefield[..., 0, :, :]
        imag_part = wavefield[..., 1, :, :]
        axis_pos = real_part.ndim + axis_neg
        new_real = real_part - sign_value * spread_taps(imag_part, chirp_taps, axis_pos)
        new_imag = imag_part + sign_value * spread_taps(real_part, chirp_taps, axis_pos)
        wavefield = jnp.stack([new_real, new_imag], axis=-3)
    return wavefield

def complex_mul(first, second):
    ar, ai = (first[..., 0, :, :], first[..., 1, :, :])
    br, bi = (second[..., 0, :, :], second[..., 1, :, :])
    return jnp.stack([ar * br - ai * bi, ar * bi + ai * br], axis=-3)

def conj_mul(first, second):
    ar, ai = (first[..., 0, :, :], first[..., 1, :, :])
    br, bi = (second[..., 0, :, :], second[..., 1, :, :])
    return jnp.stack([ar * br + ai * bi, ar * bi - ai * br], axis=-3)

def group_forward(wavefield, windows, chirp_taps):
    incoming = []
    for number in range(windows.shape[1]):
        incoming.append(wavefield)
        wavefield = propagate(complex_mul(windows[:, number], wavefield), chirp_taps, 1.0)
    return (wavefield, jnp.stack(incoming, axis=1))

def group_adjoint(adjoint, windows, incoming, chirp_taps):
    terms = [None] * windows.shape[1]
    for number in reversed(range(windows.shape[1])):
        pulled = propagate(adjoint, chirp_taps, -1.0)
        terms[number] = conj_mul(incoming[:, number], pulled)
        adjoint = conj_mul(windows[:, number], pulled)
    return (adjoint, jnp.stack(terms, axis=1))

def dft_tables(length):
    indices = jnp.arange(length, dtype=jnp.int32)
    product = indices[:, None] * indices[None, :] % length
    angle = product.astype(jnp.float32) * (2.0 * math.pi / length)
    factor = 1.0 / math.sqrt(length)
    return ((jnp.cos(angle) * factor).astype(jnp.bfloat16), (jnp.sin(angle) * factor).astype(jnp.bfloat16))

def left_mul(matrix, values):
    return jnp.einsum('jk,bkl->bjl', matrix.astype(jnp.float32), values.astype(jnp.float32))

def right_mul(values, matrix):
    return jnp.einsum('bjk,kl->bjl', values.astype(jnp.float32), matrix.astype(jnp.float32))

def far_field(exit_wave, intensity, live_mask):
    cos_table, sin_table = dft_tables(exit_wave.shape[-1])
    exit_real = exit_wave[:, 0].astype(jnp.bfloat16)
    exit_imag = exit_wave[:, 1].astype(jnp.bfloat16)
    half_real = (left_mul(cos_table, exit_real) + left_mul(sin_table, exit_imag)).astype(jnp.bfloat16)
    half_imag = (left_mul(cos_table, exit_imag) - left_mul(sin_table, exit_real)).astype(jnp.bfloat16)
    far_real = right_mul(half_real, cos_table) + right_mul(half_imag, sin_table)
    far_imag = right_mul(half_imag, cos_table) - right_mul(half_real, sin_table)
    misfit = (far_real * far_real + far_imag * far_imag - intensity.astype(jnp.float32)) * live_mask[:, None, None]
    grad_real = (misfit * far_real).astype(jnp.bfloat16)
    grad_imag = (misfit * far_imag).astype(jnp.bfloat16)
    back_real = (left_mul(cos_table, grad_real) - left_mul(sin_table, grad_imag)).astype(jnp.bfloat16)
    back_imag = (left_mul(cos_table, grad_imag) + left_mul(sin_table, grad_real)).astype(jnp.bfloat16)
    adj_real = right_mul(back_real, cos_table) - right_mul(back_imag, sin_table)
    adj_imag = right_mul(back_imag, cos_table) + right_mul(back_real, sin_table)
    return jnp.stack([adj_real, adj_imag], axis=1)

def reference(transmission, chirp_taps, probe_field, records, pos_row, pos_col, counts):
    total_cols = transmission.shape[3]
    zero_index = jnp.int32(0)

    def tile_work(tile_id):
        columns = (tile_id * TW + jnp.arange(2 * TW, dtype=jnp.int32)) % total_cols
        extended = jnp.take(transmission, columns, axis=3)
        rows_here = pos_row[tile_id].astype(jnp.int32)
        cols_here = pos_col[tile_id].astype(jnp.int32)

        def window_at(row_start, col_start):
            return lax.dynamic_slice(extended, (zero_index, zero_index, row_start.astype(jnp.int32), col_start.astype(jnp.int32)), (SLICES, 2, W, W))
        windows = jax.vmap(window_at)(rows_here, cols_here).astype(jnp.float32)
        live_mask = (jnp.arange(CAP, dtype=jnp.int32) < counts[tile_id]).astype(jnp.float32)
        wavefield = jnp.broadcast_to(probe_field, (CAP, 2, W, W))
        stored = []
        for group in range(N_DEPTH):
            if group > 0:
                wavefield = lax.optimization_barrier(wavefield.astype(jnp.bfloat16)).astype(jnp.float32)
            wavefield, incoming = group_forward(wavefield, windows[:, group * SL:(group + 1) * SL], chirp_taps)
            stored.append(incoming)
        adjoint = far_field(wavefield, records[tile_id], live_mask)
        pieces = [None] * N_DEPTH
        for group in reversed(range(N_DEPTH)):
            if group < N_DEPTH - 1:
                adjoint = lax.optimization_barrier(adjoint.astype(jnp.bfloat16)).astype(jnp.float32)
            adjoint, pieces[group] = group_adjoint(adjoint, windows[:, group * SL:(group + 1) * SL], stored[group], chirp_taps)
        terms = jnp.concatenate(pieces, axis=1)
        accum = jnp.zeros((SLICES, 2, H, 2 * TW), jnp.float32)
        for slot in range(CAP):
            corner = (zero_index, zero_index, rows_here[slot].astype(jnp.int32), cols_here[slot].astype(jnp.int32))
            current = lax.dynamic_slice(accum, corner, (SLICES, 2, W, W))
            accum = lax.dynamic_update_slice(accum, current + terms[slot], corner)
        return accum
    last_accum = tile_work(jnp.int32(TILES - 1))

    def scan_step(carried, tile_id):
        accum = tile_work(tile_id)
        result = (accum[..., :TW] + carried).astype(jnp.bfloat16)
        return (accum[..., TW:], result)
    unused, tiles_out = lax.scan(scan_step, last_accum[..., TW:], jnp.arange(TILES, dtype=jnp.int32))
    return jnp.moveaxis(tiles_out, 0, 3).reshape(SLICES, 2, H, TILES * TW)
```

```python
import math

import jax
import jax.numpy as jnp
import numpy as np
from jax import lax
from jax.experimental import pallas as pl
from jax.experimental.pallas import tpu as pltpu
from jax.sharding import PartitionSpec as P

W = 256
STEP = 16
SPAN = W + STEP
LS = 16
RS = 8
EDGE = W - 8
BF = jnp.bfloat16
F32 = jnp.float32
ROW, COL, CNT, DEP = 0, 2, 4, 5


def dot(a, b):
    return jnp.dot(a, b, preferred_element_type=F32)


def iota(shape, dim):
    return lax.broadcasted_iota(jnp.int32, shape, dim)


def dft_tables():
    indices = np.arange(W)
    angle = (indices[:, None] * indices[None, :] % W).astype(np.float64) * (2.0 * math.pi / W)
    factor = 1.0 / math.sqrt(W)
    cos = (np.cos(angle) * factor).astype(np.float32)
    sin = (np.sin(angle) * factor).astype(np.float32)
    return np.concatenate([cos, sin], axis=0), np.concatenate([cos, sin], axis=1)


def place(meta, slot, height):
    row = meta[ROW + slot]
    base = jnp.minimum(row // STEP * STEP, height - SPAN)
    return base, row - base, meta[COL + slot]


def fold(buf, offset):
    lane = buf.shape[-1]
    top = jnp.where(iota((STEP, lane), 0) < offset, buf[W:SPAN].astype(F32), buf[0:STEP].astype(F32))
    return jnp.concatenate([top.astype(BF), buf[STEP:W]], axis=0)


def taps_table(taps, shift):
    a = (iota((W, W), 0) - shift) & (W - 1)
    b = (iota((W, W), 1) - shift) & (W - 1)
    k = jnp.abs(a - b)
    out = jnp.zeros((W, W), F32)
    for distance in range(5):
        out = jnp.where(k == distance, taps[distance], out)
    return out.astype(BF)


def propagate(re, im, t_row, t_col, sign):
    y = dot(jnp.concatenate([re.astype(BF), im.astype(BF)], axis=0), t_col)
    re, im = re - sign * y[W:], im + sign * y[:W]
    z = dot(t_row, jnp.concatenate([re.astype(BF), im.astype(BF)], axis=1))
    return re - sign * z[:, W:], im + sign * z[:, :W]


def one_hot(shift, transposed):
    m, a = (iota((W, W), 1), iota((W, W), 0)) if transposed else (iota((W, W), 0), iota((W, W), 1))
    return jnp.where(a == ((m - shift) & (W - 1)), 1.0, 0.0).astype(BF)


def rotate_probe(probe, row_shift, col_shift):
    re, im = probe[0], probe[1]
    hr, hi = re.astype(BF), im.astype(BF)
    lr, li = (re - hr.astype(F32)).astype(BF), (im - hi.astype(F32)).astype(BF)
    x = dot(one_hot(row_shift, False), jnp.concatenate([hr, hi, lr, li], axis=1)).astype(BF)
    y = jnp.concatenate([x[:, i * W : (i + 1) * W] for i in range(4)], axis=0)
    z = dot(y, one_hot(col_shift, True))
    return z[0:W] + z[2 * W : 3 * W], z[W : 2 * W] + z[3 * W :]


def forward(w0, w1, psi0, t_row, t_col):
    p1 = propagate(w0[0] * psi0[0] - w0[1] * psi0[1], w0[0] * psi0[1] + w0[1] * psi0[0], t_row, t_col, 1.0)
    p1b = (p1[0].astype(BF), p1[1].astype(BF))
    q = (p1b[0].astype(F32), p1b[1].astype(F32))
    p2 = propagate(w1[0] * q[0] - w1[1] * q[1], w1[0] * q[1] + w1[1] * q[0], t_row, t_col, 1.0)
    return p1b, (p2[0].astype(BF), p2[1].astype(BF))


def pack(parts, first, width):
    blocks = 128 // (width * len(parts))
    rows = W // blocks
    left = jnp.concatenate(
        [part[b * rows : (b + 1) * rows] for b in range(blocks) for part in parts], axis=1
    )
    q = iota((left.shape[1], 128), 0)
    lane = iota((left.shape[1], 128), 1)
    col = (q & 127) - first
    hit = (col >= 0) & (col < width) & (lane == (q // 128) * width + col)
    return dot(left, jnp.where(hit, 1.0, 0.0).astype(BF)).astype(BF)


def unpack(packed, count, first, width):
    blocks = 128 // (width * count)
    n = blocks * count * 128
    q = iota((128, n), 1)
    lane = iota((128, n), 0)
    col = (q & 127) - first
    hit = (col >= 0) & (col < width) & (lane == (q // 128) * width + col)
    out = dot(packed, jnp.where(hit, 1.0, 0.0).astype(BF)).astype(BF)
    return [
        jnp.concatenate(
            [out[:, (b * count + i) * 128 : (b * count + i + 1) * 128] for b in range(blocks)], axis=0
        )
        for i in range(count)
    ]


def span_copy(tile, base, buf, sem):
    return pltpu.make_async_copy(tile.at[0, :, pl.ds(base, SPAN), :], buf, sem)


def left_windows(meta, tile, keep, send, strip_keep, strip_send, buf, sems):
    height = tile.shape[2]
    mine = meta[DEP]
    copies = []
    for k, slot in enumerate((mine, 1 - mine)):
        base, _, _ = place(meta, slot, height)
        copy = span_copy(tile, pl.multiple_of(base, STEP), buf.at[k], sems.at[k])
        copy.start()
        copies.append(copy)
    for k, (slot, out, strip) in enumerate(((1 - mine, send, strip_send), (mine, keep, strip_keep))):
        copies[1 - k].wait()
        _, offset, _ = place(meta, slot, height)
        parts = []
        for i in range(2):
            window = fold(buf[1 - k, i], offset)
            out[i] = window
            parts.append(window[:, W - 128 :])
        strip[...] = pack(parts, 128 - LS, LS)


def pair(own, other, mine):
    first = jnp.where(mine == 0, own, other)
    second = jnp.where(mine == 0, other, own)
    return first, second


def left_forward(meta, taps, keep, recv, probe, exit_ref, psi0_ref, t_row_ref, t_col_ref):
    mine = meta[DEP]
    _, offset, col0 = place(meta, mine, meta[DEP + 1])
    t_row, t_col = taps_table(taps, offset), taps_table(taps, col0)
    t_row_ref[...], t_col_ref[...] = t_row, t_col
    psi0 = rotate_probe(probe, offset, col0)
    psi0_ref[0], psi0_ref[1] = psi0
    inside = iota((W, W), 1) >= col0
    own = [jnp.where(inside, keep[i].astype(F32), 0.0) for i in range(2)]
    other = [jnp.where(inside, recv[i].astype(F32), 0.0) for i in range(2)]
    re, im = pair(own[0], other[0], mine), pair(own[1], other[1], mine)
    _, psi2 = forward((re[0], im[0]), (re[1], im[1]), psi0, t_row, t_col)
    exit_ref[0], exit_ref[1] = psi2


def right_forward(
    meta, taps, tile, tile_other, strip_a, strip_b, probe,
    exit_ref, strip_out, w_ref, psi0_ref, psi1_ref, t_row_ref, t_col_ref, buf, sems,
):
    mine = meta[DEP]
    base, offset, col0 = place(meta, mine, tile.shape[2])
    base = pl.multiple_of(base, STEP)
    copies = [
        span_copy(tile, base, buf.at[mine], sems.at[0]),
        span_copy(tile_other, base, buf.at[1 - mine], sems.at[1]),
    ]
    for copy in copies:
        copy.start()
    t_row, t_col = taps_table(taps, offset), taps_table(taps, col0)
    t_row_ref[...], t_col_ref[...] = t_row, t_col
    psi0 = rotate_probe(probe, offset, col0)
    psi0_ref[0], psi0_ref[1] = psi0
    lane = iota((W, 128), 1)
    strips = pair(strip_a[...].astype(F32), strip_b[...].astype(F32), mine)
    for copy in copies:
        copy.wait()
    windows, heads = [], []
    for s in range(2):
        left = unpack(strips[s].astype(BF), 2, 128 - LS, LS)
        for i in range(2):
            window = fold(buf[s, i], offset)
            heads.append(window[:, :128])
            w_ref[s, i, :, :128] = jnp.where(lane < col0, window[:, :128].astype(F32), 0.0).astype(BF)
            w_ref[s, i, :, 128:] = jnp.where(
                lane + 128 < col0, window[:, 128:].astype(F32), left[i].astype(F32)
            ).astype(BF)
            windows.append(w_ref[s, i].astype(F32))
    strip_out[...] = pack(heads, 0, RS)
    psi1, psi2 = forward(windows[0:2], windows[2:4], psi0, t_row, t_col)
    psi1_ref[0], psi1_ref[1] = psi1
    exit_ref[0], exit_ref[1] = psi2


def left_merge(meta, keep, recv, strip, psi0, t_row, t_col, w_ref, psi1_ref):
    mine = meta[DEP]
    _, _, col0 = place(meta, mine, meta[DEP + 1])
    heads = unpack(strip[...], 4, 0, RS)
    lane = iota((W, 128), 1)
    for i in range(2):
        parts = pair(keep[i].astype(F32), recv[i].astype(F32), mine)
        for s in range(2):
            w_ref[s, i, :, :128] = jnp.where(lane >= col0, parts[s][:, :128], heads[s * 2 + i].astype(F32)).astype(BF)
            w_ref[s, i, :, 128:] = jnp.where(lane + 128 >= col0, parts[s][:, 128:], 0.0).astype(BF)
    w = (w_ref[0, 0].astype(F32), w_ref[0, 1].astype(F32))
    p1 = propagate(
        w[0] * psi0[0] - w[1] * psi0[1], w[0] * psi0[1] + w[1] * psi0[0], t_row[...], t_col[...], 1.0
    )
    psi1_ref[0], psi1_ref[1] = p1[0].astype(BF), p1[1].astype(BF)


def rotated_tables(meta, tall, wide, f_row, f_col_t, f_row_t, f_col):
    _, offset, col0 = place(meta, meta[DEP], meta[DEP + 1])
    f_row[...] = dot(one_hot(offset, False), wide[...]).astype(BF)
    x = dot(tall[...], one_hot(offset, True)).astype(BF)
    f_row_t[:, :W], f_row_t[:, W:] = x[:W], x[W:]
    f_col_t[...] = dot(tall[...], one_hot(col0, True)).astype(BF)
    y = dot(one_hot(col0, False), wide[...]).astype(BF)
    f_col[:W], f_col[W:] = y[:, :W], y[:, W:]


def far_field(side, meta, exit_l, exit_r, record, f_row, f_col_t, f_row_t, f_col, w, psi0, psi1, t_row, t_col, keep, send):
    mine = meta[DEP]
    _, _, col0 = place(meta, mine, meta[DEP + 1])
    live = jnp.where(mine < meta[CNT], 1.0, 0.0)
    column = iota((W, W), 1)
    left = (column >= col0) & (column < EDGE)
    er = jnp.where(left, exit_l[0].astype(F32), exit_r[0].astype(F32))
    ei = jnp.where(left, exit_l[1].astype(F32), exit_r[1].astype(F32))
    rhs = jnp.concatenate(
        [jnp.concatenate([er, ei], axis=1), jnp.concatenate([ei, -er], axis=1)], axis=0
    ).astype(BF)
    a = dot(f_row_t[...], rhs)
    ar, ai = a[:, :W], a[:, W:]
    lhs = jnp.concatenate(
        [jnp.concatenate([ar, ai], axis=1), jnp.concatenate([ai, -ar], axis=1)], axis=0
    ).astype(BF)
    far = dot(lhs, f_col[...])
    fr, fi = far[:W], far[W:]
    misfit = (fr * fr + fi * fi - record[...].astype(F32)) * live
    gr, gi = misfit * fr, misfit * fi
    rhs = jnp.concatenate(
        [jnp.concatenate([gr, gi], axis=1), jnp.concatenate([-gi, gr], axis=1)], axis=0
    ).astype(BF)
    b = dot(f_row[...], rhs)
    br, bi = b[:, :W], b[:, W:]
    lhs = jnp.concatenate(
        [jnp.concatenate([br, -bi], axis=1), jnp.concatenate([bi, br], axis=1)], axis=0
    ).astype(BF)
    chi = dot(lhs, f_col_t[...])
    q1 = propagate(chi[:W], chi[W:], t_row[...], t_col[...], -1.0)
    region = (column >= col0) if side == 0 else (column < col0)

    def term(psi_r, psi_i, q):
        return (
            jnp.where(region, psi_r * q[0] + psi_i * q[1], 0.0),
            jnp.where(region, psi_r * q[1] - psi_i * q[0], 0.0),
        )

    term1 = term(psi1[0].astype(F32), psi1[1].astype(F32), q1)
    wr, wi = w[1, 0].astype(F32), w[1, 1].astype(F32)
    cr = (wr * q1[0] + wi * q1[1]).astype(BF).astype(F32)
    ci = (wr * q1[1] - wi * q1[0]).astype(BF).astype(F32)
    q0 = propagate(cr, ci, t_row[...], t_col[...], -1.0)
    term0 = term(psi0[0], psi0[1], q0)
    for i in range(2):
        first, second = pair(term0[i], term1[i], mine)
        keep[i], send[i] = first.astype(BF), second.astype(BF)


def assemble(meta, meta_left, l_keep, l_recv, r_keep, r_recv, out):
    height = out.shape[2]
    out[...] = jnp.zeros(out.shape, BF)
    mine = meta[DEP]
    for where, slot, term in (
        (meta_left, mine, r_keep),
        (meta_left, 1 - mine, r_recv),
        (meta, mine, l_keep),
        (meta, 1 - mine, l_recv),
    ):
        base, offset, _ = place(where, slot, height)
        base = pl.multiple_of(base, STEP)
        mask = iota((STEP, W), 0) >= offset
        for i in range(2):
            top = term[i, 0:STEP].astype(F32)
            rows = pl.ds(base, STEP)
            out[0, i, rows, :] = (out[0, i, rows, :].astype(F32) + jnp.where(mask, top, 0.0)).astype(BF)
            rows = pl.ds(pl.multiple_of(base + STEP, STEP), W - STEP)
            out[0, i, rows, :] = (out[0, i, rows, :].astype(F32) + term[i, STEP:W].astype(F32)).astype(BF)
            rows = pl.ds(pl.multiple_of(base + W, STEP), STEP)
            out[0, i, rows, :] = (out[0, i, rows, :].astype(F32) + jnp.where(mask, 0.0, top)).astype(BF)


SMEM = pl.BlockSpec(memory_space=pltpu.SMEM)
VMEM = pl.BlockSpec(memory_space=pltpu.VMEM)
ANY = pl.BlockSpec(memory_space=pl.ANY)


def call(kernel, name, specs, outs, args, scratch=(), flops=0):
    outs = [jax.ShapeDtypeStruct(shape, kind) for shape, kind in outs]
    moved = sum(math.prod(o.shape) * o.dtype.itemsize for o in outs)
    moved += sum(math.prod(a.shape) * a.dtype.itemsize for a, s in zip(args, specs) if s is not ANY)
    return pl.pallas_call(
        kernel,
        name=name,
        out_shape=outs,
        in_specs=list(specs),
        out_specs=[VMEM] * len(outs),
        scratch_shapes=list(scratch),
        compiler_params=pltpu.CompilerParams(vmem_limit_bytes=40 * 1024 * 1024),
        cost_estimate=pl.CostEstimate(flops=flops, bytes_accessed=moved, transcendentals=0),
    )(*args)


def on_device(transmission, chirp_taps, probe_field, records, pos_row, pos_col, counts):
    height = transmission.shape[2]
    tiles = lax.axis_size("tile")
    my_depth = lax.axis_index("depth").astype(jnp.int32)

    def to_right(x):
        return lax.ppermute(x, "tile", [(i, (i + 1) % tiles) for i in range(tiles)])

    def to_left(x):
        return lax.ppermute(x, "tile", [(i, (i - 1) % tiles) for i in range(tiles)])

    def to_right_other(x):
        pairs = [(d * tiles + i, (1 - d) * tiles + (i + 1) % tiles) for d in range(2) for i in range(tiles)]
        return lax.ppermute(x, ("depth", "tile"), pairs)

    def to_other(x):
        return lax.ppermute(x, "depth", [(0, 1), (1, 0)])

    meta = jnp.concatenate(
        [pos_row[0], pos_col[0], counts, my_depth[None], jnp.full((1,), height, jnp.int32)]
    )
    meta_left = to_right(meta)
    field, strip, table = ((2, W, W), BF), ((W // 4, 128), BF), ((W, 2 * W), BF)
    tall_table, taps_shape, wave = ((2 * W, W), BF), ((W, W), BF), ((2, W, W), F32)
    windows = ((2, 2, W, W), BF)
    spans = [pltpu.VMEM((2, 2, SPAN, W), BF), pltpu.SemaphoreType.DMA((2,))]

    keep, send, strip_keep, strip_send = call(
        left_windows, "left_windows", [SMEM, ANY], [field, field, strip, strip], [meta, transmission], spans
    )
    strip_a = to_right(strip_keep)
    strip_b = to_right_other(strip_send)
    recv = to_other(send)
    record = lax.dynamic_index_in_dim(records[0], my_depth, 0, keepdims=False)
    record_left = to_right(record)
    other_tile = to_other(transmission)
    tall, wide = dft_tables()
    tall, wide = jnp.asarray(tall, BF), jnp.asarray(wide, BF)

    exit_l, psi0, t_row, t_col = call(
        left_forward, "left_forward", [SMEM, SMEM, VMEM, VMEM, VMEM],
        [field, wave, taps_shape, taps_shape], [meta, chirp_taps, keep, recv, probe_field], flops=10**9,
    )
    exit_l_left = to_right(exit_l)
    exit_r_left, strip_r_left, w_left, psi0_left, psi1_left, t_row_left, t_col_left = call(
        right_forward, "right_forward", [SMEM, SMEM, ANY, ANY, VMEM, VMEM, VMEM],
        [field, strip, windows, wave, field, taps_shape, taps_shape],
        [meta_left, chirp_taps, transmission, other_tile, strip_a, strip_b, probe_field], spans, flops=10**9,
    )
    strip_r = to_left(strip_r_left)
    exit_r = to_left(exit_r_left)
    tables = call(
        rotated_tables, "tables", [SMEM, VMEM, VMEM], [table, taps_shape_tall(), table, tall_table],
        [meta, tall, wide], flops=3 * 10**8,
    )
    tables_left = call(
        rotated_tables, "tables_left", [SMEM, VMEM, VMEM], [table, taps_shape_tall(), table, tall_table],
        [meta_left, tall, wide], flops=3 * 10**8,
    )
    w, psi1 = call(
        left_merge, "left_merge", [SMEM] + [VMEM] * 6, [windows, field],
        [meta, keep, recv, strip_r, psi0, t_row, t_col], flops=3 * 10**8,
    )

    def terms(side, *args):
        def kernel(*refs):
            far_field(side, *refs)

        return call(kernel, f"far_field_{side}", [SMEM] + [VMEM] * (len(args) - 1), [field, field], args, flops=10**9)

    r_keep, r_send = terms(
        1, meta_left, exit_l_left, exit_r_left, record_left, *tables_left,
        w_left, psi0_left, psi1_left, t_row_left, t_col_left,
    )
    r_recv = to_other(r_send)
    l_keep, l_send = terms(0, meta, exit_l, exit_r, record, *tables, w, psi0, psi1, t_row, t_col)
    l_recv = to_other(l_send)
    return call(
        assemble, "assemble", [SMEM, SMEM] + [VMEM] * 4, [(transmission.shape, BF)],
        [meta, meta_left, l_keep, l_recv, r_keep, r_recv],
    )[0]


def taps_shape_tall():
    return ((2 * W, W), BF)


def solution(mesh):
    in_specs = (
        P("depth", None, None, "tile"),
        P(),
        P(),
        P("tile", None, None, None),
        P("tile", None),
        P("tile", None),
        P("tile"),
    )
    out_specs = P("depth", None, None, "tile")
    return jax.shard_map(
        on_device, mesh=mesh, in_specs=in_specs, out_specs=out_specs, check_vma=False
    )
```

```python
import math

import jax
import jax.numpy as jnp
import numpy as np
from jax import lax
from jax.experimental import pallas as pl
from jax.experimental.pallas import tpu as pltpu
from jax.sharding import PartitionSpec as P

W = 256
STEP = 16
SPAN = W + STEP
LS = 16
RS = 4
EDGE = W - 8
BF = jnp.bfloat16
F32 = jnp.float32


def dot(a, b):
    return jnp.dot(a, b, preferred_element_type=F32)


def iota(shape, dim):
    return lax.broadcasted_iota(jnp.int32, shape, dim)


def dft_tables():
    indices = np.arange(W)
    angle = (indices[:, None] * indices[None, :] % W).astype(np.float64) * (2.0 * math.pi / W)
    factor = 1.0 / math.sqrt(W)
    cos = (np.cos(angle) * factor).astype(np.float32)
    sin = (np.sin(angle) * factor).astype(np.float32)
    return np.concatenate([cos, sin], axis=0)


def place(slots, slot):
    if len(slots) == 2:
        return slots[0][0, slot], slots[1][0, slot]
    value = slots[0][slot]
    return value & 2047, value >> 11


def span(row, height):
    base = jnp.minimum(row & ~(STEP - 1), height - SPAN)
    return pl.multiple_of(base, STEP), row - base


def fold(buf, offset):
    lane = buf.shape[-1]
    top = jnp.where(iota((STEP, lane), 0) < offset, buf[W:SPAN].astype(F32), buf[0:STEP].astype(F32))
    return jnp.concatenate([top, buf[STEP:W].astype(F32)], axis=0)


def taps_table(taps, shift):
    a = (iota((W, 1), 0) - shift) & (W - 1)
    b = (iota((1, W), 1) - shift) & (W - 1)
    k = jnp.abs(a - b)
    out = jnp.where(k == 0, taps[0], 0.0)
    for distance in range(1, 5):
        out = jnp.where(k == distance, taps[distance], out)
    return out.astype(BF)


def column_pass(re, im, t_col, sign):
    y = dot(jnp.concatenate([re.astype(BF), im.astype(BF)], axis=0), t_col)
    return re - sign * y[W:], im + sign * y[:W]


def propagate(re, im, t_row, t_col, sign):
    re, im = column_pass(re, im, t_col, sign)
    z = dot(t_row, jnp.concatenate([re.astype(BF), im.astype(BF)], axis=1))
    return re - sign * z[:, W:], im + sign * z[:, :W]


def one_hot(shift, transposed):
    if transposed:
        hit = iota((W, 1), 0) == ((iota((1, W), 1) - shift) & (W - 1))
    else:
        hit = iota((1, W), 1) == ((iota((W, 1), 0) - shift) & (W - 1))
    return jnp.where(hit, 1.0, 0.0).astype(BF)


def rotate_probe(probe, from_row, to_col):
    re, im = probe[0], probe[1]
    hr, hi = re.astype(BF), im.astype(BF)
    lr, li = (re - hr.astype(F32)).astype(BF), (im - hi.astype(F32)).astype(BF)
    x = dot(from_row, jnp.concatenate([hr, hi, lr, li], axis=1)).astype(BF)
    y = jnp.concatenate([x[:, i * W : (i + 1) * W] for i in range(4)], axis=0)
    z = dot(y, to_col)
    return z[0:W] + z[2 * W : 3 * W], z[W : 2 * W] + z[3 * W :]


def forward(w0, w1, psi0, t_row, t_col):
    p1 = propagate(w0[0] * psi0[0] - w0[1] * psi0[1], w0[0] * psi0[1] + w0[1] * psi0[0], t_row, t_col, 1.0)
    p1b = (p1[0].astype(BF), p1[1].astype(BF))
    q = (p1b[0].astype(F32), p1b[1].astype(F32))
    p2 = column_pass(w1[0] * q[0] - w1[1] * q[1], w1[0] * q[1] + w1[1] * q[0], t_col, 1.0)
    return p1b, (p2[0].astype(BF), p2[1].astype(BF))


def pack(parts, firsts, width):
    total = width * len(parts)
    blocks = 128 // total
    rows = W // blocks
    lane = iota((W, 128), 1)
    row = parts[0] if firsts[0] == 0 else pltpu.roll(parts[0], 128 - firsts[0], 1)
    for i in range(1, len(parts)):
        row = jnp.where(lane < i * width, row, pltpu.roll(parts[i], (i * width - firsts[i]) % 128, 1))
    out = row[:rows]
    for b in range(1, blocks):
        moved = pltpu.roll(row[b * rows : (b + 1) * rows], b * total, 1)
        out = jnp.where(lane[:rows] < b * total, out, moved)
    return out.astype(BF)


def unpack(packed, firsts, width):
    total = width * len(firsts)
    blocks = 128 // total
    values = packed.astype(F32)
    row = jnp.concatenate(
        [values] + [pltpu.roll(values, 128 - b * total, 1) for b in range(1, blocks)], axis=0
    )
    shifts = [(first - i * width) % 128 for i, first in enumerate(firsts)]
    return [pltpu.roll(row, shift, 1) if shift else row for shift in shifts]


def pair(own, other, mine):
    return jnp.where(mine == 0, own, other), jnp.where(mine == 0, other, own)


def windows_of(tile, other, mine, base, offset):
    rows = pl.ds(base, SPAN)
    out = []
    for i in range(2):
        for s, part in enumerate(pair(fold(tile[0, i, rows, :], offset), fold(other[0, i, rows, :], offset), mine)):
            out.append((s, i, part))
    return {(s, i): part for s, i, part in out}


def edges(pos_row, pos_col, tile, records, strip_keep, strip_send, keep, buf, buf_send, sems):
    mine = lax.axis_index("depth")
    work = []
    for k, (slot, target, width) in enumerate(((mine, buf, W), (1 - mine, buf_send, 128))):
        base, offset = span(pos_row[0, slot], tile.shape[2])
        source = tile.at[0, :, pl.ds(base, SPAN), pl.ds(W - width, width)]
        copy = pltpu.make_async_copy(source, target, sems.at[k])
        copy.start()
        work.append((copy, offset))
    record_copies = []
    for half in range(2):
        source = records.at[0, 1 - mine, :, pl.ds(half * 128, 128)]
        target = strip_send.at[pl.ds(W // 4 + half * W, W), :]
        record_copies.append(pltpu.make_async_copy(source, target, sems.at[2 + half]))
        record_copies[-1].start()
    lane = iota((STEP, 128), 1)
    numbers = jnp.zeros((STEP, 128), jnp.int32)
    for slot in range(2):
        row, col = pos_row[0, slot], pos_col[0, slot]
        for k, part in enumerate((row & (W - 1), row >> 8, col)):
            numbers = jnp.where(lane == slot * 4 + k, part, numbers)
    strip_keep[W // 4 :] = numbers.astype(F32).astype(BF)
    (copy, offset), (copy_send, offset_send) = work
    copy.wait()
    window = [fold(buf[i], offset) for i in range(2)]
    keep[0], keep[1] = window[0].astype(BF), window[1].astype(BF)
    strip_keep[: W // 4] = pack([part[:, W - 128 :] for part in window], [128 - LS] * 2, LS)
    copy_send.wait()
    strip_send[: W // 4] = pack([fold(buf_send[i], offset_send) for i in range(2)], [128 - LS] * 2, LS)
    for copy in record_copies:
        copy.wait()


def receive(strip, slots):
    lane = iota((8, 128), 1)
    values = strip[W // 4 :].astype(F32)[:8]
    for slot in range(2):
        weight = jnp.zeros((8, 128), F32)
        for k, factor in enumerate((1, W, 2048)):
            weight = jnp.where(lane == slot * 4 + k, factor / 8.0, weight)
        slots[slot] = jnp.sum(values * weight).astype(jnp.int32)


def settle(height, slots, taps, probe, psi0, t_row, t_col):
    row, col0 = place(slots, lax.axis_index("depth"))
    _, offset = span(row, height)
    t_row[...], t_col[...] = taps_table(taps, offset), taps_table(taps, col0)
    psi0[0], psi0[1] = rotate_probe(probe, one_hot(offset, False), one_hot(col0, True))


def tables(height, slots, dft, t_row, t_col, f_to, f_right, f_back, f_last):
    row, col0 = place(slots, lax.axis_index("depth"))
    _, offset = span(row, height)
    tall = dft[...]
    wide = jnp.concatenate([tall[:W], tall[W:]], axis=1)
    x = dot(tall, one_hot(offset, True)).astype(BF)
    y = dot(x, t_row[...])
    cos, sin = (x[:W].astype(F32) + y[W:]).astype(BF), (x[W:].astype(F32) - y[:W]).astype(BF)
    f_to[:W, :W], f_to[:W, W:], f_to[W:, :W], f_to[W:, W:] = cos, sin, -sin, cos
    x = dot(one_hot(col0, False), wide).astype(BF)
    cos, sin = x[:, :W], x[:, W:]
    f_right[:W, :W], f_right[:W, W:], f_right[W:, :W], f_right[W:, W:] = cos, -sin, sin, cos
    x = dot(one_hot(offset, False), wide).astype(BF)
    y = dot(t_row[...], x)
    cos, sin = (x[:, :W].astype(F32) + y[:, W:]).astype(BF), (x[:, W:].astype(F32) - y[:, :W]).astype(BF)
    f_back[:W, :W], f_back[:W, W:], f_back[W:, :W], f_back[W:, W:] = cos, -sin, sin, cos
    x = dot(tall, one_hot(col0, True)).astype(BF)
    y = dot(x, t_col[...])
    cos, sin = (x[:W].astype(F32) + y[W:]).astype(BF), (x[W:].astype(F32) - y[:W]).astype(BF)
    f_last[:W, :W], f_last[:W, W:], f_last[W:, :W], f_last[W:, W:] = cos, sin, -sin, cos


def put_exit(exit_ref, psi2, inside):
    for i in range(2):
        part = jnp.where(inside, psi2[i], 0.0).astype(BF)
        for half in range(2):
            exit_ref[(2 * i + half) * W : (2 * i + half + 1) * W] = part[:, half * 128 : (half + 1) * 128]


def left_forward(slots, counts, keep, other, psi0, t_row, t_col, exit_ref, w_ref, psi1_ref):
    mine = lax.axis_index("depth")
    row, col0 = place(slots, mine)
    base, offset = span(row, other.shape[2])
    column = iota((1, W), 1)
    inside = column >= col0
    w = {}
    for i in range(2):
        far = fold(other[0, i, pl.ds(base, SPAN), :], offset)
        for s, part in enumerate(pair(keep[i].astype(F32), far, mine)):
            w[s, i] = jnp.where(inside, part, 0.0)
    w_ref[0], w_ref[1] = w[1, 0].astype(BF), w[1, 1].astype(BF)
    psi1, psi2 = forward((w[0, 0], w[0, 1]), (w[1, 0], w[1, 1]), psi0, t_row[...], t_col[...])
    psi1_ref[0], psi1_ref[1] = psi1
    put_exit(exit_ref, psi2, inside & (column < EDGE))
    number, lane = iota((STEP, 128), 0), iota((STEP, 128), 1)
    live = jnp.where(mine < counts[0], 1.0, 0.0)
    marks = jnp.where(lane + jnp.where(number == 2, 128, 0) >= col0, 1.0, 0.0)
    exit_ref[4 * W :] = jnp.where(number == 0, live, marks).astype(BF)


def right_forward(
    slots, tile, other, strip_a, strip_b, psi0, t_row, t_col, exit_ref, w_ref, psi1_ref
):
    mine = lax.axis_index("depth")
    row, col0 = place(slots, mine)
    base, offset = span(row, tile.shape[2])
    lane, column = iota((1, 128), 1), iota((1, W), 1)
    strips = pair(strip_a[: W // 4].astype(F32), strip_b[: W // 4].astype(F32), mine)
    w = windows_of(tile, other, mine, base, offset)
    for s in range(2):
        lefts = unpack(strips[s], [128 - LS] * 2, LS)
        for i in range(2):
            left = jnp.where(lane >= 128 - LS, lefts[i], 0.0)
            low = jnp.where(lane < col0, w[s, i][:, :128], 0.0)
            high = jnp.where(lane + 128 < col0, w[s, i][:, 128:], left)
            w[s, i] = jnp.concatenate([low, high], axis=1)
    w_ref[0], w_ref[1] = w[1, 0].astype(BF), w[1, 1].astype(BF)
    psi1, psi2 = forward((w[0, 0], w[0, 1]), (w[1, 0], w[1, 1]), psi0, t_row[...], t_col[...])
    psi1_ref[0], psi1_ref[1] = psi1
    put_exit(exit_ref, psi2, (column < col0) | (column >= EDGE))
    parts = [psi1[0][:, 128:].astype(F32), psi1[1][:, 128:].astype(F32), w[1, 0][:, :128], w[1, 1][:, :128]]
    exit_ref[4 * W :] = pack(parts, [128 - RS, 128 - RS, 0, 0], RS)


def far_field(
    side, exit_l, exit_r, record, psi0, t_row, t_col, f_to, f_right, f_back, f_last, psi1, w1, keep, send
):
    mine = lax.axis_index("depth")
    notes = exit_l[4 * W :].astype(F32)
    live = notes[0:1, 0:1]
    of_left = jnp.concatenate([notes[1:2], notes[2:3]], axis=1)
    region = of_left if side == 0 else 1.0 - of_left
    lane = iota((1, 128), 1)
    halves = [exit_l[k * W : (k + 1) * W] + exit_r[k * W : (k + 1) * W] for k in range(4)]
    wave = jnp.concatenate([jnp.concatenate(halves[:2], axis=1), jnp.concatenate(halves[2:], axis=1)], axis=0)
    x = dot(f_to[...], wave).astype(BF)
    x = dot(jnp.concatenate([x[:W], x[W:]], axis=1), f_right[...])
    fr, fi = x[:, :W], x[:, W:]
    if side == 1:
        record = jnp.concatenate([record[W // 4 : W // 4 + W], record[W // 4 + W :]], axis=1)
    misfit = (fr * fr + fi * fi - record[...].astype(F32)) * live
    x = dot(f_back[...], jnp.concatenate([(misfit * fr).astype(BF), (misfit * fi).astype(BF)], axis=0)).astype(BF)
    x = dot(jnp.concatenate([x[:W], x[W:]], axis=1), f_last[...])
    q1 = x[:, :W], x[:, W:]
    psi = [psi1[i].astype(F32) for i in range(2)]
    w = [w1[i].astype(F32) for i in range(2)]
    if side == 0:
        strips = unpack(exit_r[4 * W :], [128 - RS, 128 - RS, 0, 0], RS)
        for i in range(2):
            high = jnp.where(lane >= 128 - RS, strips[i], psi[i][:, 128:])
            psi[i] = jnp.concatenate([psi[i][:, :128], high], axis=1)
            low = jnp.where(lane < RS, w[i][:, :128] + strips[2 + i] * (1.0 - of_left[:, :128]), w[i][:, :128])
            w[i] = jnp.concatenate([low, w[i][:, 128:]], axis=1)

    def term(psi_r, psi_i, q):
        return (psi_r * q[0] + psi_i * q[1]) * region, (psi_r * q[1] - psi_i * q[0]) * region

    term1 = term(psi[0], psi[1], q1)
    cr = (w[0] * q1[0] + w[1] * q1[1]).astype(BF).astype(F32)
    ci = (w[0] * q1[1] - w[1] * q1[0]).astype(BF).astype(F32)
    q0 = propagate(cr, ci, t_row[...], t_col[...], -1.0)
    term0 = term(psi0[0], psi0[1], q0)
    for i in range(2):
        first, second = pair(term0[i], term1[i], mine)
        keep[i], send[i] = first.astype(BF), second.astype(BF)


def assemble(own, left, l_keep, l_recv, r_keep, r_recv, out, buf, sems):
    height = out.shape[2]
    mine = lax.axis_index("depth")
    work = []
    for where, slot, term in (
        (left, mine, r_keep),
        (left, 1 - mine, r_recv),
        (own, mine, l_keep),
        (own, 1 - mine, l_recv),
    ):
        row, _ = place(where, slot)
        base, offset = span(row, height)
        work.append((base, offset, term))
    copies = []
    for i in range(2):
        buf[i] = jnp.zeros((height, W), BF)
        for base, offset, term in work:
            mask = iota((STEP, 1), 0) >= offset
            top = term[i, 0:STEP].astype(F32)
            rows = pl.ds(base, STEP)
            buf[i, rows, :] = buf[i, rows, :] + jnp.where(mask, top, 0.0).astype(BF)
            rows = pl.ds(pl.multiple_of(base + STEP, STEP), W - STEP)
            buf[i, rows, :] = buf[i, rows, :] + term[i, STEP:W]
            rows = pl.ds(pl.multiple_of(base + W, STEP), STEP)
            buf[i, rows, :] = buf[i, rows, :] + jnp.where(mask, 0.0, top).astype(BF)
        for k in range(4):
            rows = pl.ds(k * (height // 4), height // 4)
            copy = pltpu.make_async_copy(buf.at[i, rows, :], out.at[0, i, rows, :], sems.at[i, k])
            copy.start()
            copies.append(copy)
    for copy in copies:
        copy.wait()


SMEM = pl.BlockSpec(memory_space=pltpu.SMEM)
VMEM = pl.BlockSpec(memory_space=pltpu.VMEM)
HBM = pl.BlockSpec(memory_space=pltpu.HBM)


def call(kernel, name, specs, outs, args, scratch=(), out_specs=None, vmem=40, after=(), token=False):
    count, extra, made = len(args), len(after), len(outs)

    def body(*refs):
        refs = list(refs)
        if token:
            refs.pop(count + extra + made)[...] = jnp.zeros((8, 128), F32)
        kernel(*refs[:count], *refs[count + extra :])

    outs, out_specs = list(outs), list(out_specs or [VMEM] * made)
    if token:
        outs, out_specs = outs + [((8, 128), F32)], out_specs + [VMEM]
    moved = sum(math.prod(shape) * jnp.dtype(kind).itemsize for shape, kind in outs)
    moved += sum(math.prod(a.shape) * a.dtype.itemsize for a, s in zip(args, specs) if s is not HBM)
    return pl.pallas_call(
        body,
        name=name,
        out_shape=[jax.ShapeDtypeStruct(shape, kind) for shape, kind in outs],
        in_specs=list(specs) + [VMEM] * extra,
        out_specs=out_specs,
        scratch_shapes=list(scratch),
        compiler_params=pltpu.CompilerParams(vmem_limit_bytes=vmem * 1024 * 1024),
        cost_estimate=pl.CostEstimate(flops=10**9, bytes_accessed=moved, transcendentals=0),
    )(*args, *after)


FIELD, WAVE = ((2, W, W), BF), ((2, W, W), F32)
BAND, QUAD = ((W, W), BF), ((2 * W, 2 * W), BF)
MARKED, LOADED, SLOTS = ((W // 4 + STEP, 128), BF), ((W // 4 + 2 * W, 128), BF), ((2,), jnp.int32)
EXIT_L, EXIT_R = ((4 * W + STEP, 128), BF), ((4 * W + W * 4 * RS // 128, 128), BF)


def on_device(transmission, chirp_taps, probe_field, records, pos_row, pos_col, counts):
    height = transmission.shape[2]
    tiles = lax.axis_size("tile")
    my_depth = lax.axis_index("depth")

    def to_right(x):
        return lax.ppermute(x, "tile", [(i, (i + 1) % tiles) for i in range(tiles)])

    def to_left(x):
        return lax.ppermute(x, "tile", [(i, (i - 1) % tiles) for i in range(tiles)])

    def to_right_other(x):
        pairs = [(d * tiles + i, (1 - d) * tiles + (i + 1) % tiles) for d in range(2) for i in range(tiles)]
        return lax.ppermute(x, ("depth", "tile"), pairs)

    def to_other(x):
        return lax.ppermute(x, "depth", [(0, 1), (1, 0)])

    def own(kernel):
        return lambda pos_row, pos_col, *refs: kernel((pos_row, pos_col), *refs)

    def left(kernel):
        return lambda slots, *refs: kernel((slots,), *refs)

    def table_kernel(*refs):
        tables(height, *refs)

    def settle_own(*refs):
        settle(height, *refs)

    def settle_left(strip, taps, probe, slots, *refs):
        receive(strip, slots)
        settle(height, (slots,), taps, probe, *refs)

    def terms(side, *args, after=(), token=False):
        def kernel(*refs):
            far_field(side, *refs)

        return call(
            kernel, f"far_field_{side}", [VMEM] * len(args), [FIELD, FIELD], args, after=after, token=token
        )

    dft = jnp.asarray(dft_tables(), BF)
    other_tile = to_other(transmission)
    record = lax.dynamic_index_in_dim(records[0], my_depth, 0, keepdims=False)
    strip_keep, strip_send, keep = call(
        edges, "edges", [SMEM, SMEM, HBM, HBM], [MARKED, LOADED, FIELD],
        [pos_row, pos_col, transmission, records],
        [pltpu.VMEM((2, SPAN, W), BF), pltpu.VMEM((2, SPAN, 128), BF), pltpu.SemaphoreType.DMA((4,))], vmem=56,
    )
    strip_a = to_right(strip_keep)
    strip_b = to_right_other(strip_send)
    settled = call(
        own(settle_own), "settle", [SMEM, SMEM, SMEM, VMEM], [WAVE, BAND, BAND],
        [pos_row, pos_col, chirp_taps, probe_field],
    )
    exit_l, w1, psi1, done = call(
        own(left_forward), "left_forward", [SMEM] * 3 + [VMEM] * 5, [EXIT_L, FIELD, FIELD],
        [pos_row, pos_col, counts, keep, other_tile, *settled], token=True,
    )
    exit_l_left = to_right(exit_l)
    slots_left, *settled_left = call(
        settle_left, "settle_left", [VMEM, SMEM, VMEM], [SLOTS, WAVE, BAND, BAND],
        [strip_a, chirp_taps, probe_field], out_specs=[SMEM] + [VMEM] * 3, after=[done],
    )
    exit_r_left, w_left, psi1_left, done = call(
        left(right_forward), "right_forward", [SMEM] + [VMEM] * 7, [EXIT_R, FIELD, FIELD],
        [slots_left, transmission, other_tile, strip_a, strip_b, *settled_left], token=True,
    )
    exit_r = to_left(exit_r_left)
    *left_tables, done = call(
        left(table_kernel), "tables_left", [SMEM] + [VMEM] * 3, [QUAD] * 4, [slots_left, dft, *settled_left[1:]],
        after=[done], token=True,
    )
    *own_tables, done = call(
        own(table_kernel), "tables", [SMEM] * 2 + [VMEM] * 3, [QUAD] * 4, [pos_row, pos_col, dft, *settled[1:]],
        after=[done], token=True,
    )
    r_keep, r_send, done = terms(
        1, exit_l_left, exit_r_left, strip_b, *settled_left, *left_tables, psi1_left, w_left, after=[done], token=True
    )
    r_recv = to_other(r_send)
    l_keep, l_send = terms(0, exit_l, exit_r, record, *settled, *own_tables, psi1, w1, after=[done])
    l_recv = to_other(l_send)

    def assemble_kernel(pos_row, pos_col, slots, *refs):
        assemble((pos_row, pos_col), (slots,), *refs)

    return call(
        assemble_kernel, "assemble", [SMEM] * 3 + [VMEM] * 4, [(transmission.shape, BF)],
        [pos_row, pos_col, slots_left, l_keep, l_recv, r_keep, r_recv],
        [pltpu.VMEM((2, height, W), BF), pltpu.SemaphoreType.DMA((2, 4))], out_specs=[HBM],
    )[0]


def solution(mesh):
    in_specs = (
        P("depth", None, None, "tile"),
        P(),
        P(),
        P("tile", None, None, None),
        P("tile", None),
        P("tile", None),
        P("tile"),
    )
    out_specs = P("depth", None, None, "tile")
    return jax.shard_map(
        on_device, mesh=mesh, in_specs=in_specs, out_specs=out_specs, check_vma=False
    )
```

```python
import math

import jax
import jax.numpy as jnp
import numpy as np
from jax import lax
from jax.experimental import pallas as pl
from jax.experimental.pallas import tpu as pltpu
from jax.sharding import PartitionSpec as P

W = 256
STEP = 16
SPAN = W + STEP
LS = 16
RS = 4
EDGE = W - 8
BF = jnp.bfloat16
F32 = jnp.float32


def dot(a, b):
    return jnp.dot(a, b, preferred_element_type=F32)


def iota(shape, dim):
    return lax.broadcasted_iota(jnp.int32, shape, dim)


def dft_tables():
    indices = np.arange(W)
    angle = (indices[:, None] * indices[None, :] % W).astype(np.float64) * (2.0 * math.pi / W)
    factor = 1.0 / math.sqrt(W)
    cos = (np.cos(angle) * factor).astype(np.float32)
    sin = (np.sin(angle) * factor).astype(np.float32)
    return np.concatenate([cos, sin], axis=0)


def place(strip, slot):
    lane = iota((1, 128), 1)
    values = strip[W // 4 :].astype(F32)[0:1]
    row = jnp.sum(jnp.where(lane == slot * 4, values, jnp.where(lane == slot * 4 + 1, values * W, 0.0)))
    col = jnp.sum(jnp.where(lane == slot * 4 + 2, values, 0.0))
    return row.astype(jnp.int32), col.astype(jnp.int32)


def span(row, height):
    base = jnp.minimum(row & ~(STEP - 1), height - SPAN)
    return pl.multiple_of(base, STEP), row - base


def fold(buf, offset):
    lane = buf.shape[-1]
    top = jnp.where(iota((STEP, lane), 0) < offset, buf[W:SPAN].astype(F32), buf[0:STEP].astype(F32))
    return jnp.concatenate([top, buf[STEP:W].astype(F32)], axis=0)


def taps_table(taps, shift):
    a = (iota((W, 1), 0) - shift) & (W - 1)
    b = (iota((1, W), 1) - shift) & (W - 1)
    k = jnp.abs(a - b)
    out = jnp.zeros((W, W), F32)
    for distance in range(5):
        out = jnp.where(k == distance, taps[distance], out)
    return out.astype(BF)


def column_pass(re, im, t_col, sign):
    y = dot(jnp.concatenate([re.astype(BF), im.astype(BF)], axis=0), t_col)
    return re - sign * y[W:], im + sign * y[:W]


def propagate(re, im, t_row, t_col, sign):
    re, im = column_pass(re, im, t_col, sign)
    z = dot(t_row, jnp.concatenate([re.astype(BF), im.astype(BF)], axis=1))
    return re - sign * z[:, W:], im + sign * z[:, :W]


def one_hot(shift, transposed):
    if transposed:
        hit = iota((W, 1), 0) == ((iota((1, W), 1) - shift) & (W - 1))
    else:
        hit = iota((1, W), 1) == ((iota((W, 1), 0) - shift) & (W - 1))
    return jnp.where(hit, 1.0, 0.0).astype(BF)


def forward(w0, w1, psi0, t_row, t_col):
    p1 = propagate(w0[0] * psi0[0] - w0[1] * psi0[1], w0[0] * psi0[1] + w0[1] * psi0[0], t_row, t_col, 1.0)
    p1b = (p1[0].astype(BF), p1[1].astype(BF))
    q = (p1b[0].astype(F32), p1b[1].astype(F32))
    p2 = column_pass(w1[0] * q[0] - w1[1] * q[1], w1[0] * q[1] + w1[1] * q[0], t_col, 1.0)
    return p1b, (p2[0].astype(BF), p2[1].astype(BF))


def pack(parts, firsts, width):
    total = width * len(parts)
    blocks = 128 // total
    rows = W // blocks
    lane = iota((W, 128), 1)
    row = parts[0] if firsts[0] == 0 else pltpu.roll(parts[0], 128 - firsts[0], 1)
    for i in range(1, len(parts)):
        row = jnp.where(lane < i * width, row, pltpu.roll(parts[i], (i * width - firsts[i]) % 128, 1))
    out = row[:rows]
    for b in range(1, blocks):
        moved = pltpu.roll(row[b * rows : (b + 1) * rows], b * total, 1)
        out = jnp.where(lane[:rows] < b * total, out, moved)
    return out.astype(BF)


def unpack(packed, firsts, width):
    total = width * len(firsts)
    blocks = 128 // total
    values = packed.astype(F32)
    row = jnp.concatenate(
        [values] + [pltpu.roll(values, 128 - b * total, 1) for b in range(1, blocks)], axis=0
    )
    shifts = [(first - i * width) % 128 for i, first in enumerate(firsts)]
    return [pltpu.roll(row, shift, 1) if shift else row for shift in shifts]


def pair(own, other, mine):
    return jnp.where(mine == 0, own, other), jnp.where(mine == 0, other, own)


def windows_of(tile, other, mine, base, offset):
    rows = pl.ds(base, SPAN)
    out = []
    for i in range(2):
        for s, part in enumerate(pair(fold(tile[0, i, rows, :], offset), fold(other[0, i, rows, :], offset), mine)):
            out.append((s, i, part))
    return {(s, i): part for s, i, part in out}


def edges(
    pos_row, pos_col, chirp_taps, tile, records, strip_keep, strip_send, keep,
    rows, cols, taps, record, buf, side_buf, packed, packed_send, window, sems,
):
    mine = lax.axis_index("depth")
    height = tile.shape[2]
    pairs = [(pos_row, rows), (pos_col, cols), (chirp_taps, taps), (records.at[0, 1 - mine], record)]
    pairs += [(tile.at[0, i, :, pl.ds(W - 128, 128)], side_buf.at[i]) for i in range(2)]
    copies = [pltpu.make_async_copy(source, target, sems.at[k]) for k, (source, target) in enumerate(pairs)]
    for copy in copies:
        copy.start()
    last = []

    def put(source, target):
        last.append(pltpu.make_async_copy(source, target, sems.at[len(pairs) + 1 + len(last)]))
        last[-1].start()

    copies[0].wait()
    base, offset = span(rows[0, mine], height)
    base_send, offset_send = span(rows[0, 1 - mine], height)
    whole = pltpu.make_async_copy(tile.at[0, :, pl.ds(base, SPAN), :], buf, sems.at[len(pairs)])
    whole.start()
    copies[1].wait()
    copies[2].wait()
    lane = iota((STEP, 128), 1)
    numbers = jnp.zeros((STEP, 128), jnp.int32)
    for slot in range(2):
        row, col = rows[0, slot], cols[0, slot]
        for k, part in enumerate((row & (W - 1), row >> 8, col)):
            numbers = jnp.where(lane == slot * 4 + k, part, numbers)
    numbers = numbers.astype(F32)
    for k in range(5):
        numbers = jnp.where(lane == 8 + k, taps[k], numbers)
    packed[W // 4 :] = numbers.astype(BF)
    copies[3].wait()
    put(record, strip_send.at[W // 8 :])
    copies[4].wait()
    copies[5].wait()
    strip = pack([fold(side_buf[i, pl.ds(base_send, SPAN), :], offset_send) for i in range(2)], [128 - LS] * 2, LS)
    packed_send[...] = jnp.concatenate([strip[: W // 8], strip[W // 8 :]], axis=1)
    put(packed_send, strip_send.at[: W // 8])
    packed[: W // 4] = pack([fold(side_buf[i, pl.ds(base, SPAN), :], offset) for i in range(2)], [128 - LS] * 2, LS)
    put(packed, strip_keep)
    whole.wait()
    for i in range(2):
        window[i] = fold(buf[i], offset).astype(BF)
    put(window, keep)
    for copy in last:
        copy.wait()


def settle(taps, probe, offset, col0, psi0, t_row, t_col):
    t_row[...], t_col[...] = taps_table(taps, offset), taps_table(taps, col0)
    for i in range(2):
        psi0[i] = pltpu.roll(pltpu.roll(probe[i], offset, 0), col0, 1)


def settle_own(height, pos_row, pos_col, chirp_taps, probe, psi0, t_row, t_col, rows, cols, taps, sems):
    mine = lax.axis_index("depth")
    pairs = [(pos_row, rows), (pos_col, cols), (chirp_taps, taps)]
    copies = [pltpu.make_async_copy(source, target, sems.at[k]) for k, (source, target) in enumerate(pairs)]
    for copy in copies:
        copy.start()
    for copy in copies:
        copy.wait()
    _, offset = span(rows[0, mine], height)
    settle(taps, probe, offset, cols[0, mine], psi0, t_row, t_col)


def settle_left(height, strip, probe, psi0, t_row, t_col):
    row, col0 = place(strip, lax.axis_index("depth"))
    _, offset = span(row, height)
    numbers = strip[W // 4 :].astype(F32)[0:1]
    settle([numbers[:, 8 + k : 9 + k] for k in range(5)], probe, offset, col0, psi0, t_row, t_col)


def tables(height, strip, dft, t_row, t_col, f_to, f_right, f_back, f_last):
    row, col0 = place(strip, lax.axis_index("depth"))
    _, offset = span(row, height)
    tall = dft[...]
    wide = jnp.concatenate([tall[:W], tall[W:]], axis=1)
    x = dot(tall, one_hot(offset, True)).astype(BF)
    y = dot(x, t_row[...])
    cos, sin = (x[:W].astype(F32) + y[W:]).astype(BF), (x[W:].astype(F32) - y[:W]).astype(BF)
    f_to[:W, :W], f_to[:W, W:], f_to[W:, :W], f_to[W:, W:] = cos, sin, -sin, cos
    x = dot(one_hot(col0, False), wide).astype(BF)
    cos, sin = x[:, :W], x[:, W:]
    f_right[:W, :W], f_right[:W, W:], f_right[W:, :W], f_right[W:, W:] = cos, -sin, sin, cos
    x = dot(one_hot(offset, False), wide).astype(BF)
    y = dot(t_row[...], x)
    cos, sin = (x[:, :W].astype(F32) + y[:, W:]).astype(BF), (x[:, W:].astype(F32) - y[:, :W]).astype(BF)
    f_back[:W, :W], f_back[:W, W:], f_back[W:, :W], f_back[W:, W:] = cos, -sin, sin, cos
    x = dot(tall, one_hot(col0, True)).astype(BF)
    y = dot(x, t_col[...])
    cos, sin = (x[:W].astype(F32) + y[W:]).astype(BF), (x[W:].astype(F32) - y[:W]).astype(BF)
    f_last[:W, :W], f_last[:W, W:], f_last[W:, :W], f_last[W:, W:] = cos, sin, -sin, cos


def put_exit(exit_ref, psi2, inside):
    for i in range(2):
        part = jnp.where(inside, psi2[i], 0.0).astype(BF)
        for half in range(2):
            exit_ref[(2 * i + half) * W : (2 * i + half + 1) * W] = part[:, half * 128 : (half + 1) * 128]


def left_forward(strip, live, keep, other, psi0, t_row, t_col, exit_ref, w_ref, psi1_ref):
    mine = lax.axis_index("depth")
    row, col0 = place(strip, mine)
    base, offset = span(row, other.shape[2])
    column = iota((1, W), 1)
    inside = column >= col0
    w = {}
    for i in range(2):
        far = fold(other[0, i, pl.ds(base, SPAN), :], offset)
        for s, part in enumerate(pair(keep[i].astype(F32), far, mine)):
            w[s, i] = jnp.where(inside, part, 0.0)
    w_ref[0], w_ref[1] = w[1, 0].astype(BF), w[1, 1].astype(BF)
    psi1, psi2 = forward((w[0, 0], w[0, 1]), (w[1, 0], w[1, 1]), psi0, t_row[...], t_col[...])
    psi1_ref[0], psi1_ref[1] = psi1
    put_exit(exit_ref, psi2, inside & (column < EDGE))
    number, lane = iota((STEP, 128), 0), iota((STEP, 128), 1)
    marks = jnp.where(lane + jnp.where(number == 2, 128, 0) >= col0, 1.0, 0.0)
    exit_ref[4 * W :] = jnp.where(number == 0, live[...], marks).astype(BF)


def right_forward(
    tile, other, strip_a, strip_b, psi0, t_row, t_col, exit_ref, w_ref, psi1_ref
):
    mine = lax.axis_index("depth")
    row, col0 = place(strip_a, mine)
    base, offset = span(row, tile.shape[2])
    lane, column = iota((1, 128), 1), iota((1, W), 1)
    across = strip_b[: W // 8]
    across = jnp.concatenate([across[:, :128], across[:, 128:]], axis=0)
    strips = pair(strip_a[: W // 4].astype(F32), across.astype(F32), mine)
    w = windows_of(tile, other, mine, base, offset)
    for s in range(2):
        lefts = unpack(strips[s], [128 - LS] * 2, LS)
        for i in range(2):
            left = jnp.where(lane >= 128 - LS, lefts[i], 0.0)
            low = jnp.where(lane < col0, w[s, i][:, :128], 0.0)
            high = jnp.where(lane + 128 < col0, w[s, i][:, 128:], left)
            w[s, i] = jnp.concatenate([low, high], axis=1)
    w_ref[0], w_ref[1] = w[1, 0].astype(BF), w[1, 1].astype(BF)
    psi1, psi2 = forward((w[0, 0], w[0, 1]), (w[1, 0], w[1, 1]), psi0, t_row[...], t_col[...])
    psi1_ref[0], psi1_ref[1] = psi1
    put_exit(exit_ref, psi2, (column < col0) | (column >= EDGE))
    parts = [psi1[0][:, 128:].astype(F32), psi1[1][:, 128:].astype(F32), w[1, 0][:, :128], w[1, 1][:, :128]]
    exit_ref[4 * W :] = pack(parts, [128 - RS, 128 - RS, 0, 0], RS)


def far_field(
    side, exit_l, exit_r, record, psi0, t_row, t_col, f_to, f_right, f_back, f_last, psi1, w1, keep, send
):
    mine = lax.axis_index("depth")
    notes = exit_l[4 * W :].astype(F32)
    live = notes[0:1, 0:1]
    of_left = jnp.concatenate([notes[1:2], notes[2:3]], axis=1)
    region = of_left if side == 0 else 1.0 - of_left
    lane = iota((1, 128), 1)
    halves = [exit_l[k * W : (k + 1) * W] + exit_r[k * W : (k + 1) * W] for k in range(4)]
    wave = jnp.concatenate([jnp.concatenate(halves[:2], axis=1), jnp.concatenate(halves[2:], axis=1)], axis=0)
    x = dot(f_to[...], wave).astype(BF)
    x = dot(jnp.concatenate([x[:W], x[W:]], axis=1), f_right[...])
    fr, fi = x[:, :W], x[:, W:]
    if side == 1:
        record = record[W // 8 :]
    misfit = (fr * fr + fi * fi - record[...].astype(F32)) * live
    x = dot(f_back[...], jnp.concatenate([(misfit * fr).astype(BF), (misfit * fi).astype(BF)], axis=0)).astype(BF)
    x = dot(jnp.concatenate([x[:W], x[W:]], axis=1), f_last[...])
    q1 = x[:, :W], x[:, W:]
    psi = [psi1[i].astype(F32) for i in range(2)]
    w = [w1[i].astype(F32) for i in range(2)]
    if side == 0:
        strips = unpack(exit_r[4 * W :], [128 - RS, 128 - RS, 0, 0], RS)
        for i in range(2):
            high = jnp.where(lane >= 128 - RS, strips[i], psi[i][:, 128:])
            psi[i] = jnp.concatenate([psi[i][:, :128], high], axis=1)
            low = jnp.where(lane < RS, w[i][:, :128] + strips[2 + i] * (1.0 - of_left[:, :128]), w[i][:, :128])
            w[i] = jnp.concatenate([low, w[i][:, 128:]], axis=1)

    def term(psi_r, psi_i, q):
        return (psi_r * q[0] + psi_i * q[1]) * region, (psi_r * q[1] - psi_i * q[0]) * region

    term1 = term(psi[0], psi[1], q1)
    cr = (w[0] * q1[0] + w[1] * q1[1]).astype(BF).astype(F32)
    ci = (w[0] * q1[1] - w[1] * q1[0]).astype(BF).astype(F32)
    q0 = propagate(cr, ci, t_row[...], t_col[...], -1.0)
    term0 = term(psi0[0], psi0[1], q0)
    for i in range(2):
        first, second = pair(term0[i], term1[i], mine)
        keep[i], send[i] = first.astype(BF), second.astype(BF)


def assemble(own, left, l_keep, l_recv, r_keep, r_recv, out, buf, sems):
    height = out.shape[2]
    mine = lax.axis_index("depth")
    work = []
    for where, slot, term in (
        (left, mine, r_keep),
        (left, 1 - mine, r_recv),
        (own, mine, l_keep),
        (own, 1 - mine, l_recv),
    ):
        row, _ = place(where, slot)
        base, offset = span(row, height)
        work.append((base, offset, term))
    copies = []
    for i in range(2):
        buf[i] = jnp.zeros((height, W), BF)
        for base, offset, term in work:
            mask = iota((STEP, 1), 0) >= offset
            top = term[i, 0:STEP].astype(F32)
            rows = pl.ds(base, STEP)
            buf[i, rows, :] = buf[i, rows, :] + jnp.where(mask, top, 0.0).astype(BF)
            rows = pl.ds(pl.multiple_of(base + STEP, STEP), W - STEP)
            buf[i, rows, :] = buf[i, rows, :] + term[i, STEP:W]
            rows = pl.ds(pl.multiple_of(base + W, STEP), STEP)
            buf[i, rows, :] = buf[i, rows, :] + jnp.where(mask, 0.0, top).astype(BF)
        for k in range(4):
            rows = pl.ds(k * (height // 4), height // 4)
            copy = pltpu.make_async_copy(buf.at[i, rows, :], out.at[0, i, rows, :], sems.at[i, k])
            copy.start()
            copies.append(copy)
    for copy in copies:
        copy.wait()


VMEM = pl.BlockSpec(memory_space=pltpu.VMEM)
HBM = pl.BlockSpec(memory_space=pltpu.HBM)


def call(kernel, name, specs, outs, args, scratch=(), out_specs=None, vmem=40, after=(), token=False):
    count, extra, made = len(args), len(after), len(outs)

    def body(*refs):
        refs = list(refs)
        if token:
            refs.pop(count + extra + made)[...] = jnp.zeros((8, 128), F32)
        kernel(*refs[:count], *refs[count + extra :])

    outs, out_specs = list(outs), list(out_specs or [VMEM] * made)
    if token:
        outs, out_specs = outs + [((8, 128), F32)], out_specs + [VMEM]
    moved = sum(math.prod(shape) * jnp.dtype(kind).itemsize for shape, kind in outs)
    moved += sum(math.prod(a.shape) * a.dtype.itemsize for a, s in zip(args, specs) if s is not HBM)
    return pl.pallas_call(
        body,
        name=name,
        out_shape=[jax.ShapeDtypeStruct(shape, kind) for shape, kind in outs],
        in_specs=list(specs) + [VMEM] * extra,
        out_specs=out_specs,
        scratch_shapes=list(scratch),
        compiler_params=pltpu.CompilerParams(vmem_limit_bytes=vmem * 1024 * 1024),
        cost_estimate=pl.CostEstimate(flops=10**9, bytes_accessed=moved, transcendentals=0),
    )(*args, *after)


FIELD, WAVE = ((2, W, W), BF), ((2, W, W), F32)
BAND, QUAD = ((W, W), BF), ((2 * W, 2 * W), BF)
MARKED, LOADED = ((W // 4 + STEP, 128), BF), ((W // 8 + W, W), BF)
EXIT_L, EXIT_R = ((4 * W + STEP, 128), BF), ((4 * W + W * 4 * RS // 128, 128), BF)


def on_device(transmission, chirp_taps, probe_field, records, pos_row, pos_col, counts):
    height = transmission.shape[2]
    tiles = lax.axis_size("tile")
    my_depth = lax.axis_index("depth")

    def to_right(x):
        return lax.ppermute(x, "tile", [(i, (i + 1) % tiles) for i in range(tiles)])

    def to_left(x):
        return lax.ppermute(x, "tile", [(i, (i - 1) % tiles) for i in range(tiles)])

    def to_right_other(x):
        pairs = [(d * tiles + i, (1 - d) * tiles + (i + 1) % tiles) for d in range(2) for i in range(tiles)]
        return lax.ppermute(x, ("depth", "tile"), pairs)

    def to_other(x):
        return lax.ppermute(x, "depth", [(0, 1), (1, 0)])

    def table_kernel(*refs):
        tables(height, *refs)

    def settle_own_kernel(*refs):
        settle_own(height, *refs)

    def settle_left_kernel(*refs):
        settle_left(height, *refs)

    def terms(side, *args, after=(), token=False):
        def kernel(*refs):
            far_field(side, *refs)

        return call(
            kernel, f"far_field_{side}", [VMEM] * len(args), [FIELD, FIELD], args, after=after, token=token
        )

    dft = jnp.asarray(dft_tables(), BF)
    other_tile = to_other(transmission)
    record = lax.dynamic_index_in_dim(records[0], my_depth, 0, keepdims=False)
    scratch = [pltpu.SMEM((1, 2), jnp.int32)] * 2 + [pltpu.SMEM((5,), F32)]
    for shape in ((W, W), (2, SPAN, W), (2, height, 128), MARKED[0], (W // 8, W), (2, W, W)):
        scratch.append(pltpu.VMEM(shape, BF))
    strip_keep, strip_send, keep = call(
        edges, "edges", [HBM] * 5, [MARKED, LOADED, FIELD],
        [pos_row, pos_col, chirp_taps, transmission, records],
        scratch + [pltpu.SemaphoreType.DMA((11,))], out_specs=[HBM] * 3, vmem=56,
    )
    strip_a = to_right(strip_keep)
    strip_b = to_right_other(strip_send)
    live = jnp.broadcast_to((my_depth < counts[0]).astype(F32), (STEP, 128))
    settled = call(
        settle_own_kernel, "settle", [HBM] * 3 + [VMEM], [WAVE, BAND, BAND],
        [pos_row, pos_col, chirp_taps, probe_field], scratch[:3] + [pltpu.SemaphoreType.DMA((3,))],
    )
    exit_l, w1, psi1, done = call(
        left_forward, "left_forward", [VMEM] * 7, [EXIT_L, FIELD, FIELD],
        [strip_keep, live, keep, other_tile, *settled], token=True,
    )
    exit_l_left = to_right(exit_l)
    settled_left = call(
        settle_left_kernel, "settle_left", [VMEM] * 2, [WAVE, BAND, BAND], [strip_a, probe_field], after=[done]
    )
    exit_r_left, w_left, psi1_left, done = call(
        right_forward, "right_forward", [VMEM] * 7, [EXIT_R, FIELD, FIELD],
        [transmission, other_tile, strip_a, strip_b, *settled_left], token=True,
    )
    exit_r = to_left(exit_r_left)
    *left_tables, done = call(
        table_kernel, "tables_left", [VMEM] * 4, [QUAD] * 4, [strip_a, dft, *settled_left[1:]],
        after=[done], token=True,
    )
    *own_tables, done = call(
        table_kernel, "tables", [VMEM] * 4, [QUAD] * 4, [strip_keep, dft, *settled[1:]],
        after=[done], token=True,
    )
    r_keep, r_send, done = terms(
        1, exit_l_left, exit_r_left, strip_b, *settled_left, *left_tables, psi1_left, w_left, after=[done], token=True
    )
    r_recv = to_other(r_send)
    l_keep, l_send = terms(0, exit_l, exit_r, record, *settled, *own_tables, psi1, w1, after=[done])
    l_recv = to_other(l_send)

    return call(
        assemble, "assemble", [VMEM] * 6, [(transmission.shape, BF)],
        [strip_keep, strip_a, l_keep, l_recv, r_keep, r_recv],
        [pltpu.VMEM((2, height, W), BF), pltpu.SemaphoreType.DMA((2, 4))], out_specs=[HBM],
    )[0]


def solution(mesh):
    in_specs = (
        P("depth", None, None, "tile"),
        P(),
        P(),
        P("tile", None, None, None),
        P("tile", None),
        P("tile", None),
        P("tile"),
    )
    out_specs = P("depth", None, None, "tile")
    return jax.shard_map(
        on_device, mesh=mesh, in_specs=in_specs, out_specs=out_specs, check_vma=False
    )
```

```python
import math

import jax
import jax.numpy as jnp
import numpy as np
from jax import lax
from jax.experimental import pallas as pl
from jax.experimental.pallas import tpu as pltpu
from jax.sharding import PartitionSpec as P

W = 256
STEP = 16
SPAN = W + STEP
LS = 16
RS = 4
EARLY = 48
EDGE = W - 8
BF = jnp.bfloat16
F32 = jnp.float32


def dot(a, b):
    return jnp.dot(a, b, preferred_element_type=F32)


def iota(shape, dim):
    return lax.broadcasted_iota(jnp.int32, shape, dim)


def dft_tables():
    indices = np.arange(W)
    angle = (indices[:, None] * indices[None, :] % W).astype(np.float64) * (2.0 * math.pi / W)
    factor = 1.0 / math.sqrt(W)
    cos = (np.cos(angle) * factor).astype(np.float32)
    sin = (np.sin(angle) * factor).astype(np.float32)
    return np.concatenate([cos, sin], axis=0)


def place(strip, slot):
    lane = iota((1, 128), 1)
    values = strip[W // 4 :].astype(F32)[0:1]
    row = jnp.sum(jnp.where(lane == slot * 4, values, jnp.where(lane == slot * 4 + 1, values * W, 0.0)))
    col = jnp.sum(jnp.where(lane == slot * 4 + 2, values, 0.0))
    return row.astype(jnp.int32), col.astype(jnp.int32)


def span(row, height):
    base = jnp.minimum(row & ~(STEP - 1), height - SPAN)
    return pl.multiple_of(base, STEP), row - base


def fold(buf, offset):
    lane = buf.shape[-1]
    top = jnp.where(iota((STEP, lane), 0) < offset, buf[W:SPAN].astype(F32), buf[0:STEP].astype(F32))
    return jnp.concatenate([top, buf[STEP:W].astype(F32)], axis=0)


def taps_table(taps, shift):
    a = (iota((W, 1), 0) - shift) & (W - 1)
    b = (iota((1, W), 1) - shift) & (W - 1)
    k = jnp.abs(a - b)
    out = jnp.zeros((W, W), F32)
    for distance in range(5):
        out = jnp.where(k == distance, taps[distance], out)
    return out.astype(BF)


def column_pass(re, im, t_col, sign):
    y = dot(jnp.concatenate([re.astype(BF), im.astype(BF)], axis=0), t_col)
    return re - sign * y[W:], im + sign * y[:W]


def propagate(re, im, t_row, t_col, sign):
    re, im = column_pass(re, im, t_col, sign)
    z = dot(t_row, jnp.concatenate([re.astype(BF), im.astype(BF)], axis=1))
    return re - sign * z[:, W:], im + sign * z[:, :W]


def one_hot(shift, transposed):
    if transposed:
        hit = iota((W, 1), 0) == ((iota((1, W), 1) - shift) & (W - 1))
    else:
        hit = iota((1, W), 1) == ((iota((W, 1), 0) - shift) & (W - 1))
    return jnp.where(hit, 1.0, 0.0).astype(BF)


def forward(w0, w1, psi0, t_row, t_col):
    p1 = propagate(w0[0] * psi0[0] - w0[1] * psi0[1], w0[0] * psi0[1] + w0[1] * psi0[0], t_row, t_col, 1.0)
    p1b = (p1[0].astype(BF), p1[1].astype(BF))
    q = (p1b[0].astype(F32), p1b[1].astype(F32))
    p2 = column_pass(w1[0] * q[0] - w1[1] * q[1], w1[0] * q[1] + w1[1] * q[0], t_col, 1.0)
    return p1b, (p2[0].astype(BF), p2[1].astype(BF))


def pack(parts, firsts, width):
    total = width * len(parts)
    blocks = 128 // total
    rows = W // blocks
    lane = iota((W, 128), 1)
    row = parts[0] if firsts[0] == 0 else pltpu.roll(parts[0], 128 - firsts[0], 1)
    for i in range(1, len(parts)):
        row = jnp.where(lane < i * width, row, pltpu.roll(parts[i], (i * width - firsts[i]) % 128, 1))
    out = row[:rows]
    for b in range(1, blocks):
        moved = pltpu.roll(row[b * rows : (b + 1) * rows], b * total, 1)
        out = jnp.where(lane[:rows] < b * total, out, moved)
    return out.astype(BF)


def unpack(packed, firsts, width):
    total = width * len(firsts)
    blocks = 128 // total
    values = packed.astype(F32)
    row = jnp.concatenate(
        [values] + [pltpu.roll(values, 128 - b * total, 1) for b in range(1, blocks)], axis=0
    )
    shifts = [(first - i * width) % 128 for i, first in enumerate(firsts)]
    return [pltpu.roll(row, shift, 1) if shift else row for shift in shifts]


def pair(own, other, mine):
    return jnp.where(mine == 0, own, other), jnp.where(mine == 0, other, own)


def windows_of(tile, other, mine, base, offset):
    rows = pl.ds(base, SPAN)
    out = []
    for i in range(2):
        for s, part in enumerate(pair(fold(tile[0, i, rows, :], offset), fold(other[0, i, rows, :], offset), mine)):
            out.append((s, i, part))
    return {(s, i): part for s, i, part in out}


def edges(
    pos_row, pos_col, chirp_taps, tile, records, strip_keep, strip_send, keep,
    rows, cols, taps, record, buf, side_buf, packed, packed_send, window, sems,
):
    mine = lax.axis_index("depth")
    height = tile.shape[2]
    pairs = [(pos_row, rows), (pos_col, cols), (chirp_taps, taps), (records.at[0, 1 - mine, EARLY:], record)]
    pairs += [(tile.at[0, i, :, pl.ds(W - 128, 128)], side_buf.at[i]) for i in range(2)]
    copies = [pltpu.make_async_copy(source, target, sems.at[k]) for k, (source, target) in enumerate(pairs)]
    for copy in copies:
        copy.start()
    last = []

    def put(source, target):
        last.append(pltpu.make_async_copy(source, target, sems.at[len(pairs) + 1 + len(last)]))
        last[-1].start()

    copies[0].wait()
    base, offset = span(rows[0, mine], height)
    base_send, offset_send = span(rows[0, 1 - mine], height)
    whole = pltpu.make_async_copy(tile.at[0, :, pl.ds(base, SPAN), :], buf, sems.at[len(pairs)])
    whole.start()
    copies[1].wait()
    copies[2].wait()
    lane = iota((STEP, 128), 1)
    numbers = jnp.zeros((STEP, 128), jnp.int32)
    for slot in range(2):
        row, col = rows[0, slot], cols[0, slot]
        for k, part in enumerate((row & (W - 1), row >> 8, col)):
            numbers = jnp.where(lane == slot * 4 + k, part, numbers)
    numbers = numbers.astype(F32)
    for k in range(5):
        numbers = jnp.where(lane == 8 + k, taps[k], numbers)
    packed[W // 4 :] = numbers.astype(BF)
    copies[3].wait()
    put(record, strip_send.at[W // 8 :])
    copies[4].wait()
    copies[5].wait()
    strip = pack([fold(side_buf[i, pl.ds(base_send, SPAN), :], offset_send) for i in range(2)], [128 - LS] * 2, LS)
    packed_send[...] = jnp.concatenate([strip[: W // 8], strip[W // 8 :]], axis=1)
    put(packed_send, strip_send.at[: W // 8])
    packed[: W // 4] = pack([fold(side_buf[i, pl.ds(base, SPAN), :], offset) for i in range(2)], [128 - LS] * 2, LS)
    put(packed, strip_keep)
    whole.wait()
    for i in range(2):
        window[i] = fold(buf[i], offset).astype(BF)
    put(window, keep)
    for copy in last:
        copy.wait()


def settle(taps, probe, offset, col0, psi0, t_row, t_col):
    t_row[...], t_col[...] = taps_table(taps, offset), taps_table(taps, col0)
    for i in range(2):
        psi0[i] = pltpu.roll(pltpu.roll(probe[i], offset, 0), col0, 1)


def settle_own(height, pos_row, pos_col, chirp_taps, probe, psi0, t_row, t_col, rows, cols, taps, sems):
    mine = lax.axis_index("depth")
    pairs = [(pos_row, rows), (pos_col, cols), (chirp_taps, taps)]
    copies = [pltpu.make_async_copy(source, target, sems.at[k]) for k, (source, target) in enumerate(pairs)]
    for copy in copies:
        copy.start()
    for copy in copies:
        copy.wait()
    _, offset = span(rows[0, mine], height)
    settle(taps, probe, offset, cols[0, mine], psi0, t_row, t_col)


def settle_left(height, strip, probe, psi0, t_row, t_col):
    row, col0 = place(strip, lax.axis_index("depth"))
    _, offset = span(row, height)
    numbers = strip[W // 4 :].astype(F32)[0:1]
    settle([numbers[:, 8 + k : 9 + k] for k in range(5)], probe, offset, col0, psi0, t_row, t_col)


def tables(height, strip, dft, t_row, t_col, f_to, f_right, f_back, f_last):
    row, col0 = place(strip, lax.axis_index("depth"))
    _, offset = span(row, height)
    tall = dft[...]
    wide = jnp.concatenate([tall[:W], tall[W:]], axis=1)
    x = dot(tall, one_hot(offset, True)).astype(BF)
    y = dot(x, t_row[...])
    cos, sin = (x[:W].astype(F32) + y[W:]).astype(BF), (x[W:].astype(F32) - y[:W]).astype(BF)
    f_to[:W, :W], f_to[:W, W:], f_to[W:, :W], f_to[W:, W:] = cos, sin, -sin, cos
    x = dot(one_hot(col0, False), wide).astype(BF)
    cos, sin = x[:, :W], x[:, W:]
    f_right[:W, :W], f_right[:W, W:], f_right[W:, :W], f_right[W:, W:] = cos, -sin, sin, cos
    x = dot(one_hot(offset, False), wide).astype(BF)
    y = dot(t_row[...], x)
    cos, sin = (x[:, :W].astype(F32) + y[:, W:]).astype(BF), (x[:, W:].astype(F32) - y[:, :W]).astype(BF)
    f_back[:W, :W], f_back[:W, W:], f_back[W:, :W], f_back[W:, W:] = cos, -sin, sin, cos
    x = dot(tall, one_hot(col0, True)).astype(BF)
    y = dot(x, t_col[...])
    cos, sin = (x[:W].astype(F32) + y[W:]).astype(BF), (x[W:].astype(F32) - y[:W]).astype(BF)
    f_last[:W, :W], f_last[:W, W:], f_last[W:, :W], f_last[W:, W:] = cos, sin, -sin, cos


def put_exit(exit_ref, psi2, inside):
    for i in range(2):
        part = jnp.where(inside, psi2[i], 0.0).astype(BF)
        for half in range(2):
            exit_ref[(2 * i + half) * W : (2 * i + half + 1) * W] = part[:, half * 128 : (half + 1) * 128]


def left_forward(strip, live, record, keep, other, psi0, t_row, t_col, exit_ref, w_ref, psi1_ref):
    mine = lax.axis_index("depth")
    row, col0 = place(strip, mine)
    base, offset = span(row, other.shape[2])
    column = iota((1, W), 1)
    inside = column >= col0
    w = {}
    for i in range(2):
        far = fold(other[0, i, pl.ds(base, SPAN), :], offset)
        for s, part in enumerate(pair(keep[i].astype(F32), far, mine)):
            w[s, i] = jnp.where(inside, part, 0.0)
    w_ref[0], w_ref[1] = w[1, 0].astype(BF), w[1, 1].astype(BF)
    psi1, psi2 = forward((w[0, 0], w[0, 1]), (w[1, 0], w[1, 1]), psi0, t_row[...], t_col[...])
    psi1_ref[0], psi1_ref[1] = psi1
    put_exit(exit_ref, psi2, inside & (column < EDGE))
    number, lane = iota((STEP, 128), 0), iota((STEP, 128), 1)
    marks = jnp.where(lane + jnp.where(number == 2, 128, 0) >= col0, 1.0, 0.0)
    exit_ref[4 * W : 4 * W + STEP] = jnp.where(number == 0, live[...], marks).astype(BF)
    for half in range(2):
        start = 4 * W + STEP + half * EARLY
        exit_ref[start : start + EARLY] = record[:EARLY, half * 128 : (half + 1) * 128]


def right_forward(
    tile, other, strip_a, strip_b, psi0, t_row, t_col, exit_ref, w_ref, psi1_ref
):
    mine = lax.axis_index("depth")
    row, col0 = place(strip_a, mine)
    base, offset = span(row, tile.shape[2])
    lane, column = iota((1, 128), 1), iota((1, W), 1)
    across = strip_b[: W // 8]
    across = jnp.concatenate([across[:, :128], across[:, 128:]], axis=0)
    strips = pair(strip_a[: W // 4].astype(F32), across.astype(F32), mine)
    w = windows_of(tile, other, mine, base, offset)
    for s in range(2):
        lefts = unpack(strips[s], [128 - LS] * 2, LS)
        for i in range(2):
            left = jnp.where(lane >= 128 - LS, lefts[i], 0.0)
            low = jnp.where(lane < col0, w[s, i][:, :128], 0.0)
            high = jnp.where(lane + 128 < col0, w[s, i][:, 128:], left)
            w[s, i] = jnp.concatenate([low, high], axis=1)
    w_ref[0], w_ref[1] = w[1, 0].astype(BF), w[1, 1].astype(BF)
    psi1, psi2 = forward((w[0, 0], w[0, 1]), (w[1, 0], w[1, 1]), psi0, t_row[...], t_col[...])
    psi1_ref[0], psi1_ref[1] = psi1
    put_exit(exit_ref, psi2, (column < col0) | (column >= EDGE))
    parts = [psi1[0][:, 128:].astype(F32), psi1[1][:, 128:].astype(F32), w[1, 0][:, :128], w[1, 1][:, :128]]
    exit_ref[4 * W :] = pack(parts, [128 - RS, 128 - RS, 0, 0], RS)


def far_field(
    side, exit_l, exit_r, record, psi0, t_row, t_col, f_to, f_right, f_back, f_last, psi1, w1, keep, send
):
    mine = lax.axis_index("depth")
    notes = exit_l[4 * W : 4 * W + STEP].astype(F32)
    live = notes[0:1, 0:1]
    of_left = jnp.concatenate([notes[1:2], notes[2:3]], axis=1)
    region = of_left if side == 0 else 1.0 - of_left
    lane = iota((1, 128), 1)
    halves = [exit_l[k * W : (k + 1) * W] + exit_r[k * W : (k + 1) * W] for k in range(4)]
    wave = jnp.concatenate([jnp.concatenate(halves[:2], axis=1), jnp.concatenate(halves[2:], axis=1)], axis=0)
    x = dot(f_to[...], wave).astype(BF)
    x = dot(jnp.concatenate([x[:W], x[W:]], axis=1), f_right[...])
    fr, fi = x[:, :W], x[:, W:]
    if side == 1:
        early = exit_l[4 * W + STEP :]
        early = jnp.concatenate([early[:EARLY], early[EARLY:]], axis=1)
        record = jnp.concatenate([early, record[W // 8 :]], axis=0)
    misfit = (fr * fr + fi * fi - record[...].astype(F32)) * live
    x = dot(f_back[...], jnp.concatenate([(misfit * fr).astype(BF), (misfit * fi).astype(BF)], axis=0)).astype(BF)
    x = dot(jnp.concatenate([x[:W], x[W:]], axis=1), f_last[...])
    q1 = x[:, :W], x[:, W:]
    psi = [psi1[i].astype(F32) for i in range(2)]
    w = [w1[i].astype(F32) for i in range(2)]
    if side == 0:
        strips = unpack(exit_r[4 * W :], [128 - RS, 128 - RS, 0, 0], RS)
        for i in range(2):
            high = jnp.where(lane >= 128 - RS, strips[i], psi[i][:, 128:])
            psi[i] = jnp.concatenate([psi[i][:, :128], high], axis=1)
            low = jnp.where(lane < RS, w[i][:, :128] + strips[2 + i] * (1.0 - of_left[:, :128]), w[i][:, :128])
            w[i] = jnp.concatenate([low, w[i][:, 128:]], axis=1)

    def term(psi_r, psi_i, q):
        return (psi_r * q[0] + psi_i * q[1]) * region, (psi_r * q[1] - psi_i * q[0]) * region

    term1 = term(psi[0], psi[1], q1)
    cr = (w[0] * q1[0] + w[1] * q1[1]).astype(BF).astype(F32)
    ci = (w[0] * q1[1] - w[1] * q1[0]).astype(BF).astype(F32)
    q0 = propagate(cr, ci, t_row[...], t_col[...], -1.0)
    term0 = term(psi0[0], psi0[1], q0)
    for i in range(2):
        first, second = pair(term0[i], term1[i], mine)
        keep[i], send[i] = first.astype(BF), second.astype(BF)


def add_part(buf, i, base, offset, term):
    mask = iota((STEP, 1), 0) >= offset
    top = term[i, 0:STEP].astype(F32)
    rows = pl.ds(base, STEP)
    buf[i, rows, :] = buf[i, rows, :] + jnp.where(mask, top, 0.0).astype(BF)
    rows = pl.ds(base + STEP, W - STEP) if isinstance(base, int) else pl.ds(pl.multiple_of(base + STEP, STEP), W - STEP)
    buf[i, rows, :] = buf[i, rows, :] + term[i, STEP:W]
    rows = pl.ds(base + W, STEP) if isinstance(base, int) else pl.ds(pl.multiple_of(base + W, STEP), STEP)
    buf[i, rows, :] = buf[i, rows, :] + jnp.where(mask, 0.0, top).astype(BF)


def lay_out(own, left, l_keep, r_keep, r_recv, out, buf, sems):
    height = out.shape[2]
    mine = lax.axis_index("depth")
    work = []
    for where, slot, term in ((left, mine, r_keep), (left, 1 - mine, r_recv), (own, mine, l_keep)):
        row, _ = place(where, slot)
        base, offset = span(row, height)
        work.append((base, offset, term))
    copies = []
    for i in range(2):
        buf[i] = jnp.zeros((height, W), BF)
        for base, offset, term in work:
            add_part(buf, i, base, offset, term)
        for k in range(4):
            rows = pl.ds(k * (height // 4), height // 4)
            copy = pltpu.make_async_copy(buf.at[i, rows, :], out.at[0, i, rows, :], sems.at[i, k])
            copy.start()
            copies.append(copy)
    for copy in copies:
        copy.wait()


def finish(own, l_recv, laid, before, out, buf, sem):
    del before
    row, _ = place(own, 1 - lax.axis_index("depth"))
    base, offset = span(row, out.shape[2])
    rows = pl.ds(base, SPAN)
    for i in range(2):
        buf[i] = laid[i, rows, :]
        add_part(buf, i, 0, offset, l_recv)
    copy = pltpu.make_async_copy(buf, out.at[0, :, rows, :], sem)
    copy.start()
    copy.wait()


VMEM = pl.BlockSpec(memory_space=pltpu.VMEM)
HBM = pl.BlockSpec(memory_space=pltpu.HBM)


def call(kernel, name, specs, outs, args, scratch=(), out_specs=None, vmem=40, after=(), token=False, aliases=None):
    count, extra, made = len(args), len(after), len(outs)

    def body(*refs):
        refs = list(refs)
        if token:
            refs.pop(count + extra + made)[...] = jnp.zeros((8, 128), F32)
        kernel(*refs[:count], *refs[count + extra :])

    outs, out_specs = list(outs), list(out_specs or [VMEM] * made)
    if token:
        outs, out_specs = outs + [((8, 128), F32)], out_specs + [VMEM]
    moved = sum(math.prod(shape) * jnp.dtype(kind).itemsize for shape, kind in outs)
    moved += sum(math.prod(a.shape) * a.dtype.itemsize for a, s in zip(args, specs) if s is not HBM)
    return pl.pallas_call(
        body,
        name=name,
        out_shape=[jax.ShapeDtypeStruct(shape, kind) for shape, kind in outs],
        in_specs=list(specs) + [VMEM] * extra,
        out_specs=out_specs,
        scratch_shapes=list(scratch),
        input_output_aliases=aliases or {},
        compiler_params=pltpu.CompilerParams(vmem_limit_bytes=vmem * 1024 * 1024),
        cost_estimate=pl.CostEstimate(flops=10**9, bytes_accessed=moved, transcendentals=0),
    )(*args, *after)


FIELD, WAVE = ((2, W, W), BF), ((2, W, W), F32)
BAND, QUAD = ((W, W), BF), ((2 * W, 2 * W), BF)
MARKED, LOADED = ((W // 4 + STEP, 128), BF), ((W // 8 + W - EARLY, W), BF)
EXIT_L, EXIT_R = ((4 * W + STEP + 2 * EARLY, 128), BF), ((4 * W + W * 4 * RS // 128, 128), BF)


def on_device(transmission, chirp_taps, probe_field, records, pos_row, pos_col, counts):
    height = transmission.shape[2]
    tiles = lax.axis_size("tile")
    my_depth = lax.axis_index("depth")

    def to_right(x):
        return lax.ppermute(x, "tile", [(i, (i + 1) % tiles) for i in range(tiles)])

    def to_left(x):
        return lax.ppermute(x, "tile", [(i, (i - 1) % tiles) for i in range(tiles)])

    def to_right_other(x):
        pairs = [(d * tiles + i, (1 - d) * tiles + (i + 1) % tiles) for d in range(2) for i in range(tiles)]
        return lax.ppermute(x, ("depth", "tile"), pairs)

    def to_other(x):
        return lax.ppermute(x, "depth", [(0, 1), (1, 0)])

    def table_kernel(*refs):
        tables(height, *refs)

    def settle_own_kernel(*refs):
        settle_own(height, *refs)

    def settle_left_kernel(*refs):
        settle_left(height, *refs)

    def terms(side, *args, after=(), token=False):
        def kernel(*refs):
            far_field(side, *refs)

        return call(
            kernel, f"far_field_{side}", [VMEM] * len(args), [FIELD, FIELD], args, after=after, token=token
        )

    dft = jnp.asarray(dft_tables(), BF)
    other_tile = to_other(transmission)
    record = lax.dynamic_index_in_dim(records[0], my_depth, 0, keepdims=False)
    scratch = [pltpu.SMEM((1, 2), jnp.int32)] * 2 + [pltpu.SMEM((5,), F32)]
    for shape in ((W - EARLY, W), (2, SPAN, W), (2, height, 128), MARKED[0], (W // 8, W), (2, W, W)):
        scratch.append(pltpu.VMEM(shape, BF))
    strip_keep, strip_send, keep = call(
        edges, "edges", [HBM] * 5, [MARKED, LOADED, FIELD],
        [pos_row, pos_col, chirp_taps, transmission, records],
        scratch + [pltpu.SemaphoreType.DMA((11,))], out_specs=[HBM] * 3, vmem=56,
    )
    strip_a = to_right(strip_keep)
    strip_b = to_right_other(strip_send)
    live = jnp.broadcast_to((my_depth < counts[0]).astype(F32), (STEP, 128))
    settled = call(
        settle_own_kernel, "settle", [HBM] * 3 + [VMEM], [WAVE, BAND, BAND],
        [pos_row, pos_col, chirp_taps, probe_field], scratch[:3] + [pltpu.SemaphoreType.DMA((3,))],
    )
    exit_l, w1, psi1, done = call(
        left_forward, "left_forward", [VMEM] * 8, [EXIT_L, FIELD, FIELD],
        [strip_keep, live, record, keep, other_tile, *settled], token=True,
    )
    exit_l_left = to_right(exit_l)
    settled_left = call(
        settle_left_kernel, "settle_left", [VMEM] * 2, [WAVE, BAND, BAND], [strip_a, probe_field], after=[done]
    )
    exit_r_left, w_left, psi1_left, done = call(
        right_forward, "right_forward", [VMEM] * 7, [EXIT_R, FIELD, FIELD],
        [transmission, other_tile, strip_a, strip_b, *settled_left], token=True,
    )
    exit_r = to_left(exit_r_left)
    *left_tables, done = call(
        table_kernel, "tables_left", [VMEM] * 4, [QUAD] * 4, [strip_a, dft, *settled_left[1:]],
        after=[done], token=True,
    )
    *own_tables, done = call(
        table_kernel, "tables", [VMEM] * 4, [QUAD] * 4, [strip_keep, dft, *settled[1:]],
        after=[done], token=True,
    )
    r_keep, r_send, done = terms(
        1, exit_l_left, exit_r_left, strip_b, *settled_left, *left_tables, psi1_left, w_left, after=[done], token=True
    )
    r_recv = to_other(r_send)
    l_keep, l_send = terms(0, exit_l, exit_r, record, *settled, *own_tables, psi1, w1, after=[done])
    l_recv = to_other(l_send)

    laid_out, laid = call(
        lay_out, "lay_out", [VMEM] * 5, [(transmission.shape, BF), ((2, height, W), BF)],
        [strip_keep, strip_a, l_keep, r_keep, r_recv], [pltpu.SemaphoreType.DMA((2, 4))], out_specs=[HBM, VMEM],
    )
    return call(
        finish, "finish", [VMEM] * 3 + [HBM], [(transmission.shape, BF)], [strip_keep, l_recv, laid, laid_out],
        [pltpu.VMEM((2, SPAN, W), BF), pltpu.SemaphoreType.DMA], out_specs=[HBM], aliases={3: 0},
    )[0]


def solution(mesh):
    in_specs = (
        P("depth", None, None, "tile"),
        P(),
        P(),
        P("tile", None, None, None),
        P("tile", None),
        P("tile", None),
        P("tile"),
    )
    out_specs = P("depth", None, None, "tile")
    return jax.shard_map(
        on_device, mesh=mesh, in_specs=in_specs, out_specs=out_specs, check_vma=False
    )
```

```python
import math

import jax
import jax.numpy as jnp
import numpy as np
from jax import lax
from jax.experimental import pallas as pl
from jax.experimental.pallas import tpu as pltpu
from jax.sharding import PartitionSpec as P

W = 256
STEP = 16
SPAN = W + STEP
LS = 16
RS = 4
EARLY = 32
EDGE = W - 8
BF = jnp.bfloat16
F32 = jnp.float32


def dot(a, b):
    return jnp.dot(a, b, preferred_element_type=F32)


def iota(shape, dim):
    return lax.broadcasted_iota(jnp.int32, shape, dim)


def dft_tables():
    indices = np.arange(W)
    angle = (indices[:, None] * indices[None, :] % W).astype(np.float64) * (2.0 * math.pi / W)
    factor = 1.0 / math.sqrt(W)
    cos = (np.cos(angle) * factor).astype(np.float32)
    sin = (np.sin(angle) * factor).astype(np.float32)
    return np.concatenate([cos, sin], axis=0)


def place(strip, slot):
    lane = iota((1, 128), 1)
    values = strip[W // 4 :].astype(F32)[0:1]
    row = jnp.sum(jnp.where(lane == slot * 4, values, jnp.where(lane == slot * 4 + 1, values * W, 0.0)))
    col = jnp.sum(jnp.where(lane == slot * 4 + 2, values, 0.0))
    return row.astype(jnp.int32), col.astype(jnp.int32)


def span(row, height):
    base = jnp.minimum(row & ~(STEP - 1), height - SPAN)
    return pl.multiple_of(base, STEP), row - base


def fold(buf, offset):
    lane = buf.shape[-1]
    top = jnp.where(iota((STEP, lane), 0) < offset, buf[W:SPAN].astype(F32), buf[0:STEP].astype(F32))
    return jnp.concatenate([top, buf[STEP:W].astype(F32)], axis=0)


def taps_table(taps, shift):
    a = (iota((W, 1), 0) - shift) & (W - 1)
    b = (iota((1, W), 1) - shift) & (W - 1)
    k = jnp.abs(a - b)
    out = jnp.zeros((W, W), F32)
    for distance in range(5):
        out = jnp.where(k == distance, taps[distance], out)
    return out.astype(BF)


def column_pass(re, im, t_col, sign):
    y = dot(jnp.concatenate([re.astype(BF), im.astype(BF)], axis=0), t_col)
    return re - sign * y[W:], im + sign * y[:W]


def propagate(re, im, t_row, t_col, sign):
    re, im = column_pass(re, im, t_col, sign)
    z = dot(t_row, jnp.concatenate([re.astype(BF), im.astype(BF)], axis=1))
    return re - sign * z[:, W:], im + sign * z[:, :W]


def one_hot(shift, transposed):
    if transposed:
        hit = iota((W, 1), 0) == ((iota((1, W), 1) - shift) & (W - 1))
    else:
        hit = iota((1, W), 1) == ((iota((W, 1), 0) - shift) & (W - 1))
    return jnp.where(hit, 1.0, 0.0).astype(BF)


def forward(w0, w1, psi0, t_row, t_col):
    p1 = propagate(w0[0] * psi0[0] - w0[1] * psi0[1], w0[0] * psi0[1] + w0[1] * psi0[0], t_row, t_col, 1.0)
    p1b = (p1[0].astype(BF), p1[1].astype(BF))
    q = (p1b[0].astype(F32), p1b[1].astype(F32))
    p2 = column_pass(w1[0] * q[0] - w1[1] * q[1], w1[0] * q[1] + w1[1] * q[0], t_col, 1.0)
    return p1b, (p2[0].astype(BF), p2[1].astype(BF))


def pack(parts, firsts, width):
    total = width * len(parts)
    blocks = 128 // total
    rows = W // blocks
    lane = iota((W, 128), 1)
    row = parts[0] if firsts[0] == 0 else pltpu.roll(parts[0], 128 - firsts[0], 1)
    for i in range(1, len(parts)):
        row = jnp.where(lane < i * width, row, pltpu.roll(parts[i], (i * width - firsts[i]) % 128, 1))
    out = row[:rows]
    for b in range(1, blocks):
        moved = pltpu.roll(row[b * rows : (b + 1) * rows], b * total, 1)
        out = jnp.where(lane[:rows] < b * total, out, moved)
    return out.astype(BF)


def unpack(packed, firsts, width):
    total = width * len(firsts)
    blocks = 128 // total
    values = packed.astype(F32)
    row = jnp.concatenate(
        [values] + [pltpu.roll(values, 128 - b * total, 1) for b in range(1, blocks)], axis=0
    )
    shifts = [(first - i * width) % 128 for i, first in enumerate(firsts)]
    return [pltpu.roll(row, shift, 1) if shift else row for shift in shifts]


def pair(own, other, mine):
    return jnp.where(mine == 0, own, other), jnp.where(mine == 0, other, own)


def windows_of(tile, other, mine, base, offset):
    rows = pl.ds(base, SPAN)
    out = []
    for i in range(2):
        for s, part in enumerate(pair(fold(tile[0, i, rows, :], offset), fold(other[0, i, rows, :], offset), mine)):
            out.append((s, i, part))
    return {(s, i): part for s, i, part in out}


def edges(
    pos_row, pos_col, chirp_taps, tile, records, strip_keep, strip_send,
    rows, cols, taps, record, side_buf, packed, packed_send, sems,
):
    mine = lax.axis_index("depth")
    height = tile.shape[2]
    pairs = [(pos_row, rows), (pos_col, cols), (chirp_taps, taps), (records.at[0, 1 - mine, EARLY:], record)]
    pairs += [(tile.at[0, i, :, pl.ds(W - 128, 128)], side_buf.at[i]) for i in range(2)]
    copies = [pltpu.make_async_copy(source, target, sems.at[k]) for k, (source, target) in enumerate(pairs)]
    for copy in copies:
        copy.start()
    last = []

    def put(source, target):
        last.append(pltpu.make_async_copy(source, target, sems.at[len(pairs) + len(last)]))
        last[-1].start()

    copies[0].wait()
    base, offset = span(rows[0, mine], height)
    base_send, offset_send = span(rows[0, 1 - mine], height)
    copies[1].wait()
    copies[2].wait()
    lane = iota((STEP, 128), 1)
    numbers = jnp.zeros((STEP, 128), jnp.int32)
    for slot in range(2):
        row, col = rows[0, slot], cols[0, slot]
        for k, part in enumerate((row & (W - 1), row >> 8, col)):
            numbers = jnp.where(lane == slot * 4 + k, part, numbers)
    numbers = numbers.astype(F32)
    for k in range(5):
        numbers = jnp.where(lane == 8 + k, taps[k], numbers)
    packed[W // 4 :] = numbers.astype(BF)
    copies[3].wait()
    put(record, strip_send.at[W // 8 :])
    copies[4].wait()
    copies[5].wait()
    strip = pack([fold(side_buf[i, pl.ds(base_send, SPAN), :], offset_send) for i in range(2)], [128 - LS] * 2, LS)
    packed_send[...] = jnp.concatenate([strip[: W // 8], strip[W // 8 :]], axis=1)
    put(packed_send, strip_send.at[: W // 8])
    packed[: W // 4] = pack([fold(side_buf[i, pl.ds(base, SPAN), :], offset) for i in range(2)], [128 - LS] * 2, LS)
    put(packed, strip_keep)
    for copy in last:
        copy.wait()


def settle(taps, probe, offset, col0, psi0, t_row, t_col):
    t_row[...], t_col[...] = taps_table(taps, offset), taps_table(taps, col0)
    for i in range(2):
        psi0[i] = pltpu.roll(pltpu.roll(probe[i], offset, 0), col0, 1)


def settle_own(pos_row, pos_col, chirp_taps, tile, probe, keep, psi0, t_row, t_col, rows, cols, taps, buf, sems):
    mine = lax.axis_index("depth")
    pairs = [(pos_row, rows), (pos_col, cols), (chirp_taps, taps)]
    copies = [pltpu.make_async_copy(source, target, sems.at[k]) for k, (source, target) in enumerate(pairs)]
    for copy in copies:
        copy.start()
    copies[0].wait()
    base, offset = span(rows[0, mine], tile.shape[2])
    whole = pltpu.make_async_copy(tile.at[0, :, pl.ds(base, SPAN), :], buf, sems.at[3])
    whole.start()
    copies[1].wait()
    copies[2].wait()
    settle(taps, probe, offset, cols[0, mine], psi0, t_row, t_col)
    whole.wait()
    for i in range(2):
        keep[i] = fold(buf[i], offset).astype(BF)


def settle_left(height, strip, probe, psi0, t_row, t_col):
    row, col0 = place(strip, lax.axis_index("depth"))
    _, offset = span(row, height)
    numbers = strip[W // 4 :].astype(F32)[0:1]
    settle([numbers[:, 8 + k : 9 + k] for k in range(5)], probe, offset, col0, psi0, t_row, t_col)


def tables(height, strip, dft, t_row, t_col, f_to, f_right, f_back, f_last):
    row, col0 = place(strip, lax.axis_index("depth"))
    _, offset = span(row, height)
    tall = dft[...]
    wide = jnp.concatenate([tall[:W], tall[W:]], axis=1)
    x = dot(tall, one_hot(offset, True)).astype(BF)
    y = dot(x, t_row[...])
    cos, sin = (x[:W].astype(F32) + y[W:]).astype(BF), (x[W:].astype(F32) - y[:W]).astype(BF)
    f_to[:W, :W], f_to[:W, W:], f_to[W:, :W], f_to[W:, W:] = cos, sin, -sin, cos
    x = dot(one_hot(col0, False), wide).astype(BF)
    cos, sin = x[:, :W], x[:, W:]
    f_right[:W, :W], f_right[:W, W:], f_right[W:, :W], f_right[W:, W:] = cos, -sin, sin, cos
    x = dot(one_hot(offset, False), wide).astype(BF)
    y = dot(t_row[...], x)
    cos, sin = (x[:, :W].astype(F32) + y[:, W:]).astype(BF), (x[:, W:].astype(F32) - y[:, :W]).astype(BF)
    f_back[:W, :W], f_back[:W, W:], f_back[W:, :W], f_back[W:, W:] = cos, -sin, sin, cos
    x = dot(tall, one_hot(col0, True)).astype(BF)
    y = dot(x, t_col[...])
    cos, sin = (x[:W].astype(F32) + y[W:]).astype(BF), (x[W:].astype(F32) - y[:W]).astype(BF)
    f_last[:W, :W], f_last[:W, W:], f_last[W:, :W], f_last[W:, W:] = cos, sin, -sin, cos


def put_exit(exit_ref, psi2, inside):
    for i in range(2):
        part = jnp.where(inside, psi2[i], 0.0).astype(BF)
        for half in range(2):
            exit_ref[(2 * i + half) * W : (2 * i + half + 1) * W] = part[:, half * 128 : (half + 1) * 128]


def left_forward(strip, live, record, keep, other, psi0, t_row, t_col, exit_ref, w_ref, psi1_ref):
    mine = lax.axis_index("depth")
    row, col0 = place(strip, mine)
    base, offset = span(row, other.shape[2])
    column = iota((1, W), 1)
    inside = column >= col0
    w = {}
    for i in range(2):
        far = fold(other[0, i, pl.ds(base, SPAN), :], offset)
        for s, part in enumerate(pair(keep[i].astype(F32), far, mine)):
            w[s, i] = jnp.where(inside, part, 0.0)
    w_ref[0], w_ref[1] = w[1, 0].astype(BF), w[1, 1].astype(BF)
    psi1, psi2 = forward((w[0, 0], w[0, 1]), (w[1, 0], w[1, 1]), psi0, t_row[...], t_col[...])
    psi1_ref[0], psi1_ref[1] = psi1
    put_exit(exit_ref, psi2, inside & (column < EDGE))
    number, lane = iota((STEP, 128), 0), iota((STEP, 128), 1)
    marks = jnp.where(lane + jnp.where(number == 2, 128, 0) >= col0, 1.0, 0.0)
    exit_ref[4 * W : 4 * W + STEP] = jnp.where(number == 0, live[...], marks).astype(BF)
    for half in range(2):
        start = 4 * W + STEP + half * EARLY
        exit_ref[start : start + EARLY] = record[:EARLY, half * 128 : (half + 1) * 128]


def right_forward(
    tile, other, strip_a, strip_b, psi0, t_row, t_col, exit_ref, w_ref, psi1_ref
):
    mine = lax.axis_index("depth")
    row, col0 = place(strip_a, mine)
    base, offset = span(row, tile.shape[2])
    lane, column = iota((1, 128), 1), iota((1, W), 1)
    across = strip_b[: W // 8]
    across = jnp.concatenate([across[:, :128], across[:, 128:]], axis=0)
    strips = pair(strip_a[: W // 4].astype(F32), across.astype(F32), mine)
    w = windows_of(tile, other, mine, base, offset)
    for s in range(2):
        lefts = unpack(strips[s], [128 - LS] * 2, LS)
        for i in range(2):
            left = jnp.where(lane >= 128 - LS, lefts[i], 0.0)
            low = jnp.where(lane < col0, w[s, i][:, :128], 0.0)
            high = jnp.where(lane + 128 < col0, w[s, i][:, 128:], left)
            w[s, i] = jnp.concatenate([low, high], axis=1)
    w_ref[0], w_ref[1] = w[1, 0].astype(BF), w[1, 1].astype(BF)
    psi1, psi2 = forward((w[0, 0], w[0, 1]), (w[1, 0], w[1, 1]), psi0, t_row[...], t_col[...])
    psi1_ref[0], psi1_ref[1] = psi1
    put_exit(exit_ref, psi2, (column < col0) | (column >= EDGE))
    parts = [psi1[0][:, 128:].astype(F32), psi1[1][:, 128:].astype(F32), w[1, 0][:, :128], w[1, 1][:, :128]]
    exit_ref[4 * W :] = pack(parts, [128 - RS, 128 - RS, 0, 0], RS)


def far_field(
    side, exit_l, exit_r, record, psi0, t_row, t_col, f_to, f_right, f_back, f_last, psi1, w1, keep, send
):
    mine = lax.axis_index("depth")
    notes = exit_l[4 * W : 4 * W + STEP].astype(F32)
    live = notes[0:1, 0:1]
    of_left = jnp.concatenate([notes[1:2], notes[2:3]], axis=1)
    region = of_left if side == 0 else 1.0 - of_left
    lane = iota((1, 128), 1)
    halves = [exit_l[k * W : (k + 1) * W] + exit_r[k * W : (k + 1) * W] for k in range(4)]
    wave = jnp.concatenate([jnp.concatenate(halves[:2], axis=1), jnp.concatenate(halves[2:], axis=1)], axis=0)
    x = dot(f_to[...], wave).astype(BF)
    x = dot(jnp.concatenate([x[:W], x[W:]], axis=1), f_right[...])
    fr, fi = x[:, :W], x[:, W:]
    if side == 1:
        early = exit_l[4 * W + STEP :]
        early = jnp.concatenate([early[:EARLY], early[EARLY:]], axis=1)
        record = jnp.concatenate([early, record[W // 8 :]], axis=0)
    misfit = (fr * fr + fi * fi - record[...].astype(F32)) * live
    x = dot(f_back[...], jnp.concatenate([(misfit * fr).astype(BF), (misfit * fi).astype(BF)], axis=0)).astype(BF)
    x = dot(jnp.concatenate([x[:W], x[W:]], axis=1), f_last[...])
    q1 = x[:, :W], x[:, W:]
    psi = [psi1[i].astype(F32) for i in range(2)]
    w = [w1[i].astype(F32) for i in range(2)]
    if side == 0:
        strips = unpack(exit_r[4 * W :], [128 - RS, 128 - RS, 0, 0], RS)
        for i in range(2):
            high = jnp.where(lane >= 128 - RS, strips[i], psi[i][:, 128:])
            psi[i] = jnp.concatenate([psi[i][:, :128], high], axis=1)
            low = jnp.where(lane < RS, w[i][:, :128] + strips[2 + i] * (1.0 - of_left[:, :128]), w[i][:, :128])
            w[i] = jnp.concatenate([low, w[i][:, 128:]], axis=1)

    def term(psi_r, psi_i, q):
        return (psi_r * q[0] + psi_i * q[1]) * region, (psi_r * q[1] - psi_i * q[0]) * region

    term1 = term(psi[0], psi[1], q1)
    cr = (w[0] * q1[0] + w[1] * q1[1]).astype(BF).astype(F32)
    ci = (w[0] * q1[1] - w[1] * q1[0]).astype(BF).astype(F32)
    q0 = propagate(cr, ci, t_row[...], t_col[...], -1.0)
    term0 = term(psi0[0], psi0[1], q0)
    for i in range(2):
        first, second = pair(term0[i], term1[i], mine)
        keep[i], send[i] = first.astype(BF), second.astype(BF)


def add_part(buf, i, base, offset, term):
    mask = iota((STEP, 1), 0) >= offset
    top = term[i, 0:STEP].astype(F32)
    rows = pl.ds(base, STEP)
    buf[i, rows, :] = buf[i, rows, :] + jnp.where(mask, top, 0.0).astype(BF)
    rows = pl.ds(base + STEP, W - STEP) if isinstance(base, int) else pl.ds(pl.multiple_of(base + STEP, STEP), W - STEP)
    buf[i, rows, :] = buf[i, rows, :] + term[i, STEP:W]
    rows = pl.ds(base + W, STEP) if isinstance(base, int) else pl.ds(pl.multiple_of(base + W, STEP), STEP)
    buf[i, rows, :] = buf[i, rows, :] + jnp.where(mask, 0.0, top).astype(BF)


def lay_out(own, left, l_keep, r_keep, r_recv, out, buf, sems):
    height = out.shape[2]
    mine = lax.axis_index("depth")
    work = []
    for where, slot, term in ((left, mine, r_keep), (left, 1 - mine, r_recv), (own, mine, l_keep)):
        row, _ = place(where, slot)
        base, offset = span(row, height)
        work.append((base, offset, term))
    copies = []
    for i in range(2):
        buf[i] = jnp.zeros((height, W), BF)
        for base, offset, term in work:
            add_part(buf, i, base, offset, term)
        for k in range(4):
            rows = pl.ds(k * (height // 4), height // 4)
            copy = pltpu.make_async_copy(buf.at[i, rows, :], out.at[0, i, rows, :], sems.at[i, k])
            copy.start()
            copies.append(copy)
    for copy in copies:
        copy.wait()


def finish(own, l_recv, laid, before, out, buf, sem):
    del before
    row, _ = place(own, 1 - lax.axis_index("depth"))
    base, offset = span(row, out.shape[2])
    rows = pl.ds(base, SPAN)
    for i in range(2):
        buf[i] = laid[i, rows, :]
        add_part(buf, i, 0, offset, l_recv)
    copy = pltpu.make_async_copy(buf, out.at[0, :, rows, :], sem)
    copy.start()
    copy.wait()


VMEM = pl.BlockSpec(memory_space=pltpu.VMEM)
HBM = pl.BlockSpec(memory_space=pltpu.HBM)


def call(kernel, name, specs, outs, args, scratch=(), out_specs=None, vmem=40, after=(), token=False, aliases=None):
    count, extra, made = len(args), len(after), len(outs)

    def body(*refs):
        refs = list(refs)
        if token:
            refs.pop(count + extra + made)[...] = jnp.zeros((8, 128), F32)
        kernel(*refs[:count], *refs[count + extra :])

    outs, out_specs = list(outs), list(out_specs or [VMEM] * made)
    if token:
        outs, out_specs = outs + [((8, 128), F32)], out_specs + [VMEM]
    moved = sum(math.prod(shape) * jnp.dtype(kind).itemsize for shape, kind in outs)
    moved += sum(math.prod(a.shape) * a.dtype.itemsize for a, s in zip(args, specs) if s is not HBM)
    return pl.pallas_call(
        body,
        name=name,
        out_shape=[jax.ShapeDtypeStruct(shape, kind) for shape, kind in outs],
        in_specs=list(specs) + [VMEM] * extra,
        out_specs=out_specs,
        scratch_shapes=list(scratch),
        input_output_aliases=aliases or {},
        compiler_params=pltpu.CompilerParams(vmem_limit_bytes=vmem * 1024 * 1024),
        cost_estimate=pl.CostEstimate(flops=10**9, bytes_accessed=moved, transcendentals=0),
    )(*args, *after)


FIELD, WAVE = ((2, W, W), BF), ((2, W, W), F32)
BAND, QUAD = ((W, W), BF), ((2 * W, 2 * W), BF)
MARKED, LOADED = ((W // 4 + STEP, 128), BF), ((W // 8 + W - EARLY, W), BF)
EXIT_L, EXIT_R = ((4 * W + STEP + 2 * EARLY, 128), BF), ((4 * W + W * 4 * RS // 128, 128), BF)


def on_device(transmission, chirp_taps, probe_field, records, pos_row, pos_col, counts):
    height = transmission.shape[2]
    tiles = lax.axis_size("tile")
    my_depth = lax.axis_index("depth")

    def to_right(x):
        return lax.ppermute(x, "tile", [(i, (i + 1) % tiles) for i in range(tiles)])

    def to_left(x):
        return lax.ppermute(x, "tile", [(i, (i - 1) % tiles) for i in range(tiles)])

    def to_right_other(x):
        pairs = [(d * tiles + i, (1 - d) * tiles + (i + 1) % tiles) for d in range(2) for i in range(tiles)]
        return lax.ppermute(x, ("depth", "tile"), pairs)

    def to_other(x):
        return lax.ppermute(x, "depth", [(0, 1), (1, 0)])

    def table_kernel(*refs):
        tables(height, *refs)

    def settle_left_kernel(*refs):
        settle_left(height, *refs)

    def terms(side, *args, after=(), token=False):
        def kernel(*refs):
            far_field(side, *refs)

        return call(
            kernel, f"far_field_{side}", [VMEM] * len(args), [FIELD, FIELD], args, after=after, token=token
        )

    dft = jnp.asarray(dft_tables(), BF)
    other_tile = to_other(transmission)
    record = lax.dynamic_index_in_dim(records[0], my_depth, 0, keepdims=False)
    scalars = [pltpu.SMEM((1, 2), jnp.int32)] * 2 + [pltpu.SMEM((5,), F32)]
    shapes = (W - EARLY, W), (2, height, 128), MARKED[0], (W // 8, W)
    strip_keep, strip_send = call(
        edges, "edges", [HBM] * 5, [MARKED, LOADED], [pos_row, pos_col, chirp_taps, transmission, records],
        scalars + [pltpu.VMEM(shape, BF) for shape in shapes] + [pltpu.SemaphoreType.DMA((9,))],
        out_specs=[HBM] * 2, vmem=56,
    )
    strip_a = to_right(strip_keep)
    strip_b = to_right_other(strip_send)
    live = jnp.broadcast_to((my_depth < counts[0]).astype(F32), (STEP, 128))
    keep, *settled = call(
        settle_own, "settle", [HBM] * 4 + [VMEM], [FIELD, WAVE, BAND, BAND],
        [pos_row, pos_col, chirp_taps, transmission, probe_field],
        scalars + [pltpu.VMEM((2, SPAN, W), BF), pltpu.SemaphoreType.DMA((4,))], vmem=51,
    )
    exit_l, w1, psi1, done = call(
        left_forward, "left_forward", [VMEM] * 8, [EXIT_L, FIELD, FIELD],
        [strip_keep, live, record, keep, other_tile, *settled], token=True,
    )
    exit_l_left = to_right(exit_l)
    settled_left = call(
        settle_left_kernel, "settle_left", [VMEM] * 2, [WAVE, BAND, BAND], [strip_a, probe_field], after=[done]
    )
    exit_r_left, w_left, psi1_left, done = call(
        right_forward, "right_forward", [VMEM] * 7, [EXIT_R, FIELD, FIELD],
        [transmission, other_tile, strip_a, strip_b, *settled_left], token=True,
    )
    exit_r = to_left(exit_r_left)
    *left_tables, done = call(
        table_kernel, "tables_left", [VMEM] * 4, [QUAD] * 4, [strip_a, dft, *settled_left[1:]],
        after=[done], token=True,
    )
    *own_tables, done = call(
        table_kernel, "tables", [VMEM] * 4, [QUAD] * 4, [strip_keep, dft, *settled[1:]],
        after=[done], token=True,
    )
    r_keep, r_send, done = terms(
        1, exit_l_left, exit_r_left, strip_b, *settled_left, *left_tables, psi1_left, w_left, after=[done], token=True
    )
    r_recv = to_other(r_send)
    l_keep, l_send = terms(0, exit_l, exit_r, record, *settled, *own_tables, psi1, w1, after=[done])
    l_recv = to_other(l_send)

    laid_out, laid = call(
        lay_out, "lay_out", [VMEM] * 5, [(transmission.shape, BF), ((2, height, W), BF)],
        [strip_keep, strip_a, l_keep, r_keep, r_recv], [pltpu.SemaphoreType.DMA((2, 4))], out_specs=[HBM, VMEM],
    )
    return call(
        finish, "finish", [VMEM] * 3 + [HBM], [(transmission.shape, BF)], [strip_keep, l_recv, laid, laid_out],
        [pltpu.VMEM((2, SPAN, W), BF), pltpu.SemaphoreType.DMA], out_specs=[HBM], aliases={3: 0},
    )[0]


def solution(mesh):
    in_specs = (
        P("depth", None, None, "tile"),
        P(),
        P(),
        P("tile", None, None, None),
        P("tile", None),
        P("tile", None),
        P("tile"),
    )
    out_specs = P("depth", None, None, "tile")
    return jax.shard_map(
        on_device, mesh=mesh, in_specs=in_specs, out_specs=out_specs, check_vma=False
    )
```

```python
import math

import jax
import jax.numpy as jnp
import numpy as np
from jax import lax
from jax.experimental import pallas as pl
from jax.experimental.pallas import tpu as pltpu
from jax.sharding import PartitionSpec as P

W = 256
STEP = 16
SPAN = W + STEP
LS = 16
RS = 4
EARLY = 32
EDGE = W - 8
BF = jnp.bfloat16
F32 = jnp.float32


def dot(a, b):
    return jnp.dot(a, b, preferred_element_type=F32)


def iota(shape, dim):
    return lax.broadcasted_iota(jnp.int32, shape, dim)


def dft_tables():
    indices = np.arange(W)
    angle = (indices[:, None] * indices[None, :] % W).astype(np.float64) * (2.0 * math.pi / W)
    factor = 1.0 / math.sqrt(W)
    cos = (np.cos(angle) * factor).astype(np.float32)
    sin = (np.sin(angle) * factor).astype(np.float32)
    return np.concatenate([cos, sin], axis=0)


def place(strip, slot):
    lane = iota((1, 128), 1)
    values = strip[W // 4 :].astype(F32)[0:1]
    row = jnp.sum(jnp.where(lane == slot * 4, values, jnp.where(lane == slot * 4 + 1, values * W, 0.0)))
    col = jnp.sum(jnp.where(lane == slot * 4 + 2, values, 0.0))
    return row.astype(jnp.int32), col.astype(jnp.int32)


def span(row, height):
    base = jnp.minimum(row & ~(STEP - 1), height - SPAN)
    return pl.multiple_of(base, STEP), row - base


def fold(buf, offset):
    lane = buf.shape[-1]
    top = jnp.where(iota((STEP, lane), 0) < offset, buf[W:SPAN].astype(F32), buf[0:STEP].astype(F32))
    return jnp.concatenate([top, buf[STEP:W].astype(F32)], axis=0)


def taps_table(taps, shift):
    a = (iota((W, 1), 0) - shift) & (W - 1)
    b = (iota((1, W), 1) - shift) & (W - 1)
    k = jnp.abs(a - b)
    out = jnp.zeros((W, W), F32)
    for distance in range(5):
        out = jnp.where(k == distance, taps[distance], out)
    return out.astype(BF)


def column_pass(re, im, t_col, sign):
    y = dot(jnp.concatenate([re.astype(BF), im.astype(BF)], axis=0), t_col)
    return re - sign * y[W:], im + sign * y[:W]


def propagate(re, im, t_row, t_col, sign):
    re, im = column_pass(re, im, t_col, sign)
    z = dot(t_row, jnp.concatenate([re.astype(BF), im.astype(BF)], axis=1))
    return re - sign * z[:, W:], im + sign * z[:, :W]


def one_hot(shift, transposed):
    if transposed:
        hit = iota((W, 1), 0) == ((iota((1, W), 1) - shift) & (W - 1))
    else:
        hit = iota((1, W), 1) == ((iota((W, 1), 0) - shift) & (W - 1))
    return jnp.where(hit, 1.0, 0.0).astype(BF)


def forward(w0, w1, psi0, t_row, t_col):
    p1 = propagate(w0[0] * psi0[0] - w0[1] * psi0[1], w0[0] * psi0[1] + w0[1] * psi0[0], t_row, t_col, 1.0)
    p1b = (p1[0].astype(BF), p1[1].astype(BF))
    q = (p1b[0].astype(F32), p1b[1].astype(F32))
    p2 = column_pass(w1[0] * q[0] - w1[1] * q[1], w1[0] * q[1] + w1[1] * q[0], t_col, 1.0)
    return p1b, (p2[0].astype(BF), p2[1].astype(BF))


def pack(parts, firsts, width):
    total = width * len(parts)
    blocks = 128 // total
    rows = W // blocks
    lane = iota((W, 128), 1)
    row = parts[0] if firsts[0] == 0 else pltpu.roll(parts[0], 128 - firsts[0], 1)
    for i in range(1, len(parts)):
        row = jnp.where(lane < i * width, row, pltpu.roll(parts[i], (i * width - firsts[i]) % 128, 1))
    out = row[:rows]
    for b in range(1, blocks):
        moved = pltpu.roll(row[b * rows : (b + 1) * rows], b * total, 1)
        out = jnp.where(lane[:rows] < b * total, out, moved)
    return out.astype(BF)


def unpack(packed, firsts, width):
    total = width * len(firsts)
    blocks = 128 // total
    values = packed.astype(F32)
    row = jnp.concatenate(
        [values] + [pltpu.roll(values, 128 - b * total, 1) for b in range(1, blocks)], axis=0
    )
    shifts = [(first - i * width) % 128 for i, first in enumerate(firsts)]
    return [pltpu.roll(row, shift, 1) if shift else row for shift in shifts]


def pair(own, other, mine):
    return jnp.where(mine == 0, own, other), jnp.where(mine == 0, other, own)


def windows_of(tile, other, mine, base, offset):
    rows = pl.ds(base, SPAN)
    out = []
    for i in range(2):
        for s, part in enumerate(pair(fold(tile[0, i, rows, :], offset), fold(other[0, i, rows, :], offset), mine)):
            out.append((s, i, part))
    return {(s, i): part for s, i, part in out}


def edges(
    pos_row, pos_col, chirp_taps, tile, records, strip_keep, strip_send,
    rows, cols, taps, record, side_buf, packed, packed_send, sems,
):
    mine = lax.axis_index("depth")
    height = tile.shape[2]
    pairs = [(pos_row, rows), (pos_col, cols), (chirp_taps, taps), (records.at[0, 1 - mine, EARLY:], record)]
    pairs += [(tile.at[0, i, :, pl.ds(W - 128, 128)], side_buf.at[i]) for i in range(2)]
    copies = [pltpu.make_async_copy(source, target, sems.at[k]) for k, (source, target) in enumerate(pairs)]
    for copy in copies:
        copy.start()
    last = []

    def put(source, target):
        last.append(pltpu.make_async_copy(source, target, sems.at[len(pairs) + len(last)]))
        last[-1].start()

    copies[0].wait()
    base, offset = span(rows[0, mine], height)
    base_send, offset_send = span(rows[0, 1 - mine], height)
    copies[1].wait()
    copies[2].wait()
    lane = iota((STEP, 128), 1)
    numbers = jnp.zeros((STEP, 128), jnp.int32)
    for slot in range(2):
        row, col = rows[0, slot], cols[0, slot]
        for k, part in enumerate((row & (W - 1), row >> 8, col)):
            numbers = jnp.where(lane == slot * 4 + k, part, numbers)
    numbers = numbers.astype(F32)
    for k in range(5):
        numbers = jnp.where(lane == 8 + k, taps[k], numbers)
    packed[W // 4 :] = numbers.astype(BF)
    copies[3].wait()
    put(record, strip_send.at[W // 8 :])
    copies[4].wait()
    copies[5].wait()
    strip = pack([fold(side_buf[i, pl.ds(base_send, SPAN), :], offset_send) for i in range(2)], [128 - LS] * 2, LS)
    packed_send[...] = jnp.concatenate([strip[: W // 8], strip[W // 8 :]], axis=1)
    put(packed_send, strip_send.at[: W // 8])
    packed[: W // 4] = pack([fold(side_buf[i, pl.ds(base, SPAN), :], offset) for i in range(2)], [128 - LS] * 2, LS)
    put(packed, strip_keep)
    for copy in last:
        copy.wait()


def settle(taps, probe, offset, col0, psi0, t_row, t_col):
    t_row[...], t_col[...] = taps_table(taps, offset), taps_table(taps, col0)
    for i in range(2):
        psi0[i] = pltpu.roll(pltpu.roll(probe[i], offset, 0), col0, 1)


def settle_own(pos_row, pos_col, chirp_taps, tile, probe, keep, psi0, t_row, t_col, rows, cols, taps, buf, sems):
    mine = lax.axis_index("depth")
    pairs = [(pos_row, rows), (pos_col, cols), (chirp_taps, taps)]
    copies = [pltpu.make_async_copy(source, target, sems.at[k]) for k, (source, target) in enumerate(pairs)]
    for copy in copies:
        copy.start()
    copies[0].wait()
    base, offset = span(rows[0, mine], tile.shape[2])
    whole = pltpu.make_async_copy(tile.at[0, :, pl.ds(base, SPAN), :], buf, sems.at[3])
    whole.start()
    copies[1].wait()
    copies[2].wait()
    settle(taps, probe, offset, cols[0, mine], psi0, t_row, t_col)
    whole.wait()
    for i in range(2):
        keep[i] = fold(buf[i], offset).astype(BF)


def settle_left(height, strip, probe, psi0, t_row, t_col):
    row, col0 = place(strip, lax.axis_index("depth"))
    _, offset = span(row, height)
    numbers = strip[W // 4 :].astype(F32)[0:1]
    settle([numbers[:, 8 + k : 9 + k] for k in range(5)], probe, offset, col0, psi0, t_row, t_col)


def tables(height, strip, dft, t_row, t_col, f_to, f_right, f_back, f_last):
    row, col0 = place(strip, lax.axis_index("depth"))
    _, offset = span(row, height)
    tall = dft[...]
    wide = jnp.concatenate([tall[:W], tall[W:]], axis=1)
    x = dot(tall, one_hot(offset, True)).astype(BF)
    y = dot(x, t_row[...])
    cos, sin = (x[:W].astype(F32) + y[W:]).astype(BF), (x[W:].astype(F32) - y[:W]).astype(BF)
    f_to[:W, :W], f_to[:W, W:], f_to[W:, :W], f_to[W:, W:] = cos, sin, -sin, cos
    x = dot(one_hot(col0, False), wide).astype(BF)
    cos, sin = x[:, :W], x[:, W:]
    f_right[:W, :W], f_right[:W, W:], f_right[W:, :W], f_right[W:, W:] = cos, -sin, sin, cos
    x = dot(one_hot(offset, False), wide).astype(BF)
    y = dot(t_row[...], x)
    cos, sin = (x[:, :W].astype(F32) + y[:, W:]).astype(BF), (x[:, W:].astype(F32) - y[:, :W]).astype(BF)
    f_back[:W, :W], f_back[:W, W:], f_back[W:, :W], f_back[W:, W:] = cos, -sin, sin, cos
    x = dot(tall, one_hot(col0, True)).astype(BF)
    y = dot(x, t_col[...])
    cos, sin = (x[:W].astype(F32) + y[W:]).astype(BF), (x[W:].astype(F32) - y[:W]).astype(BF)
    f_last[:W, :W], f_last[:W, W:], f_last[W:, :W], f_last[W:, W:] = cos, sin, -sin, cos


def put_exit(exit_ref, psi2, inside):
    for i in range(2):
        part = jnp.where(inside, psi2[i], 0.0).astype(BF)
        for half in range(2):
            exit_ref[(2 * i + half) * W : (2 * i + half + 1) * W] = part[:, half * 128 : (half + 1) * 128]


def left_forward(strip, live, record, keep, other, psi0, t_row, t_col, exit_ref, w_ref, psi1_ref):
    mine = lax.axis_index("depth")
    row, col0 = place(strip, mine)
    base, offset = span(row, other.shape[2])
    column = iota((1, W), 1)
    inside = column >= col0
    w = {}
    for i in range(2):
        far = fold(other[0, i, pl.ds(base, SPAN), :], offset)
        for s, part in enumerate(pair(keep[i].astype(F32), far, mine)):
            w[s, i] = jnp.where(inside, part, 0.0)
    w_ref[0], w_ref[1] = w[1, 0].astype(BF), w[1, 1].astype(BF)
    psi1, psi2 = forward((w[0, 0], w[0, 1]), (w[1, 0], w[1, 1]), psi0, t_row[...], t_col[...])
    psi1_ref[0], psi1_ref[1] = psi1
    put_exit(exit_ref, psi2, inside & (column < EDGE))
    number, lane = iota((STEP, 128), 0), iota((STEP, 128), 1)
    marks = jnp.where(lane + jnp.where(number == 2, 128, 0) >= col0, 1.0, 0.0)
    exit_ref[4 * W : 4 * W + STEP] = jnp.where(number == 0, live[...], marks).astype(BF)
    for half in range(2):
        start = 4 * W + STEP + half * EARLY
        exit_ref[start : start + EARLY] = record[:EARLY, half * 128 : (half + 1) * 128]


def right_forward(
    tile, other, strip_a, strip_b, psi0, t_row, t_col, exit_ref, w_ref, psi1_ref
):
    mine = lax.axis_index("depth")
    row, col0 = place(strip_a, mine)
    base, offset = span(row, tile.shape[2])
    lane, column = iota((1, 128), 1), iota((1, W), 1)
    across = strip_b[: W // 8]
    across = jnp.concatenate([across[:, :128], across[:, 128:]], axis=0)
    strips = pair(strip_a[: W // 4].astype(F32), across.astype(F32), mine)
    w = windows_of(tile, other, mine, base, offset)
    for s in range(2):
        lefts = unpack(strips[s], [128 - LS] * 2, LS)
        for i in range(2):
            left = jnp.where(lane >= 128 - LS, lefts[i], 0.0)
            low = jnp.where(lane < col0, w[s, i][:, :128], 0.0)
            high = jnp.where(lane + 128 < col0, w[s, i][:, 128:], left)
            w[s, i] = jnp.concatenate([low, high], axis=1)
    w_ref[0], w_ref[1] = w[1, 0].astype(BF), w[1, 1].astype(BF)
    psi1, psi2 = forward((w[0, 0], w[0, 1]), (w[1, 0], w[1, 1]), psi0, t_row[...], t_col[...])
    psi1_ref[0], psi1_ref[1] = psi1
    put_exit(exit_ref, psi2, (column < col0) | (column >= EDGE))
    parts = [psi1[0][:, 128:].astype(F32), psi1[1][:, 128:].astype(F32), w[1, 0][:, :128], w[1, 1][:, :128]]
    exit_ref[4 * W :] = pack(parts, [128 - RS, 128 - RS, 0, 0], RS)


def far_field(
    side, exit_l, exit_r, record, psi0, t_row, t_col, f_to, f_right, f_back, f_last, psi1, w1, keep, send
):
    mine = lax.axis_index("depth")
    notes = exit_l[4 * W : 4 * W + STEP].astype(F32)
    live = notes[0:1, 0:1]
    of_left = jnp.concatenate([notes[1:2], notes[2:3]], axis=1)
    region = of_left if side == 0 else 1.0 - of_left
    lane = iota((1, 128), 1)
    halves = [exit_l[k * W : (k + 1) * W] + exit_r[k * W : (k + 1) * W] for k in range(4)]
    wave = jnp.concatenate([jnp.concatenate(halves[:2], axis=1), jnp.concatenate(halves[2:], axis=1)], axis=0)
    x = dot(f_to[...], wave).astype(BF)
    x = dot(jnp.concatenate([x[:W], x[W:]], axis=1), f_right[...])
    fr, fi = x[:, :W], x[:, W:]
    if side == 1:
        early = exit_l[4 * W + STEP :]
        early = jnp.concatenate([early[:EARLY], early[EARLY:]], axis=1)
        record = jnp.concatenate([early, record[W // 8 :]], axis=0)
    misfit = (fr * fr + fi * fi - record[...].astype(F32)) * live
    x = dot(f_back[...], jnp.concatenate([(misfit * fr).astype(BF), (misfit * fi).astype(BF)], axis=0)).astype(BF)
    x = dot(jnp.concatenate([x[:W], x[W:]], axis=1), f_last[...])
    q1 = x[:, :W], x[:, W:]
    psi = [psi1[i].astype(F32) for i in range(2)]
    w = [w1[i].astype(F32) for i in range(2)]
    if side == 0:
        strips = unpack(exit_r[4 * W :], [128 - RS, 128 - RS, 0, 0], RS)
        for i in range(2):
            high = jnp.where(lane >= 128 - RS, strips[i], psi[i][:, 128:])
            psi[i] = jnp.concatenate([psi[i][:, :128], high], axis=1)
            low = jnp.where(lane < RS, w[i][:, :128] + strips[2 + i] * (1.0 - of_left[:, :128]), w[i][:, :128])
            w[i] = jnp.concatenate([low, w[i][:, 128:]], axis=1)

    def term(psi_r, psi_i, q):
        return (psi_r * q[0] + psi_i * q[1]) * region, (psi_r * q[1] - psi_i * q[0]) * region

    term1 = term(psi[0], psi[1], q1)
    cr = (w[0] * q1[0] + w[1] * q1[1]).astype(BF).astype(F32)
    ci = (w[0] * q1[1] - w[1] * q1[0]).astype(BF).astype(F32)
    q0 = propagate(cr, ci, t_row[...], t_col[...], -1.0)
    term0 = term(psi0[0], psi0[1], q0)
    for i in range(2):
        first, second = pair(term0[i], term1[i], mine)
        keep[i], send[i] = first.astype(BF), second.astype(BF)


def add_part(buf, i, base, offset, term):
    mask = iota((STEP, 1), 0) >= offset
    top = term[i, 0:STEP].astype(F32)
    rows = pl.ds(base, STEP)
    buf[i, rows, :] = buf[i, rows, :] + jnp.where(mask, top, 0.0).astype(BF)
    rows = pl.ds(base + STEP, W - STEP) if isinstance(base, int) else pl.ds(pl.multiple_of(base + STEP, STEP), W - STEP)
    buf[i, rows, :] = buf[i, rows, :] + term[i, STEP:W]
    rows = pl.ds(base + W, STEP) if isinstance(base, int) else pl.ds(pl.multiple_of(base + W, STEP), STEP)
    buf[i, rows, :] = buf[i, rows, :] + jnp.where(mask, 0.0, top).astype(BF)


def lay_out(own, left, l_keep, r_keep, r_recv, out, buf, sems):
    height = out.shape[2]
    mine = lax.axis_index("depth")
    work = []
    for where, slot, term in ((left, mine, r_keep), (left, 1 - mine, r_recv), (own, mine, l_keep)):
        row, _ = place(where, slot)
        base, offset = span(row, height)
        work.append((base, offset, term))
    copies = []
    for i in range(2):
        buf[i] = jnp.zeros((height, W), BF)
        for base, offset, term in work:
            add_part(buf, i, base, offset, term)
        copy = pltpu.make_async_copy(buf.at[i], out.at[0, i], sems.at[i])
        copy.start()
        copies.append(copy)
    for copy in copies:
        copy.wait()


def finish(own, l_recv, laid, before, out, buf, sem):
    del before
    row, _ = place(own, 1 - lax.axis_index("depth"))
    base, offset = span(row, out.shape[2])
    rows = pl.ds(base, SPAN)
    for i in range(2):
        buf[i] = laid[i, rows, :]
        add_part(buf, i, 0, offset, l_recv)
    copy = pltpu.make_async_copy(buf, out.at[0, :, rows, :], sem)
    copy.start()
    copy.wait()


VMEM = pl.BlockSpec(memory_space=pltpu.VMEM)
HBM = pl.BlockSpec(memory_space=pltpu.HBM)


def call(kernel, name, specs, outs, args, scratch=(), out_specs=None, vmem=40, after=(), token=False, aliases=None):
    count, extra, made = len(args), len(after), len(outs)

    def body(*refs):
        refs = list(refs)
        if token:
            refs.pop(count + extra + made)[...] = jnp.zeros((8, 128), F32)
        kernel(*refs[:count], *refs[count + extra :])

    outs, out_specs = list(outs), list(out_specs or [VMEM] * made)
    if token:
        outs, out_specs = outs + [((8, 128), F32)], out_specs + [VMEM]
    moved = sum(math.prod(shape) * jnp.dtype(kind).itemsize for shape, kind in outs)
    moved += sum(math.prod(a.shape) * a.dtype.itemsize for a, s in zip(args, specs) if s is not HBM)
    return pl.pallas_call(
        body,
        name=name,
        out_shape=[jax.ShapeDtypeStruct(shape, kind) for shape, kind in outs],
        in_specs=list(specs) + [VMEM] * extra,
        out_specs=out_specs,
        scratch_shapes=list(scratch),
        input_output_aliases=aliases or {},
        compiler_params=pltpu.CompilerParams(vmem_limit_bytes=vmem * 1024 * 1024),
        cost_estimate=pl.CostEstimate(flops=10**9, bytes_accessed=moved, transcendentals=0),
    )(*args, *after)


FIELD, WAVE = ((2, W, W), BF), ((2, W, W), F32)
BAND, QUAD = ((W, W), BF), ((2 * W, 2 * W), BF)
MARKED, LOADED = ((W // 4 + STEP, 128), BF), ((W // 8 + W - EARLY, W), BF)
EXIT_L, EXIT_R = ((4 * W + STEP + 2 * EARLY, 128), BF), ((4 * W + W * 4 * RS // 128, 128), BF)


def on_device(transmission, chirp_taps, probe_field, records, pos_row, pos_col, counts):
    height = transmission.shape[2]
    tiles = lax.axis_size("tile")
    my_depth = lax.axis_index("depth")

    def to_right(x):
        return lax.ppermute(x, "tile", [(i, (i + 1) % tiles) for i in range(tiles)])

    def to_left(x):
        return lax.ppermute(x, "tile", [(i, (i - 1) % tiles) for i in range(tiles)])

    def to_right_other(x):
        pairs = [(d * tiles + i, (1 - d) * tiles + (i + 1) % tiles) for d in range(2) for i in range(tiles)]
        return lax.ppermute(x, ("depth", "tile"), pairs)

    def to_other(x):
        return lax.ppermute(x, "depth", [(0, 1), (1, 0)])

    def table_kernel(*refs):
        tables(height, *refs)

    def settle_left_kernel(*refs):
        settle_left(height, *refs)

    def terms(side, *args, after=(), token=False):
        def kernel(*refs):
            far_field(side, *refs)

        return call(
            kernel, f"far_field_{side}", [VMEM] * len(args), [FIELD, FIELD], args, after=after, token=token
        )

    dft = jnp.asarray(dft_tables(), BF)
    other_tile = to_other(transmission)
    record = lax.dynamic_index_in_dim(records[0], my_depth, 0, keepdims=False)
    scalars = [pltpu.SMEM((1, 2), jnp.int32)] * 2 + [pltpu.SMEM((5,), F32)]
    shapes = (W - EARLY, W), (2, height, 128), MARKED[0], (W // 8, W)
    strip_keep, strip_send = call(
        edges, "edges", [HBM] * 5, [MARKED, LOADED], [pos_row, pos_col, chirp_taps, transmission, records],
        scalars + [pltpu.VMEM(shape, BF) for shape in shapes] + [pltpu.SemaphoreType.DMA((9,))],
        out_specs=[HBM] * 2, vmem=56,
    )
    strip_a = to_right(strip_keep)
    strip_b = to_right_other(strip_send)
    live = jnp.broadcast_to((my_depth < counts[0]).astype(F32), (STEP, 128))
    keep, *settled = call(
        settle_own, "settle", [HBM] * 4 + [VMEM], [FIELD, WAVE, BAND, BAND],
        [pos_row, pos_col, chirp_taps, transmission, probe_field],
        scalars + [pltpu.VMEM((2, SPAN, W), BF), pltpu.SemaphoreType.DMA((4,))], vmem=51,
    )
    exit_l, w1, psi1, done = call(
        left_forward, "left_forward", [VMEM] * 8, [EXIT_L, FIELD, FIELD],
        [strip_keep, live, record, keep, other_tile, *settled], token=True,
    )
    exit_l_left = to_right(exit_l)
    settled_left = call(
        settle_left_kernel, "settle_left", [VMEM] * 2, [WAVE, BAND, BAND], [strip_a, probe_field], after=[done]
    )
    exit_r_left, w_left, psi1_left, done = call(
        right_forward, "right_forward", [VMEM] * 7, [EXIT_R, FIELD, FIELD],
        [transmission, other_tile, strip_a, strip_b, *settled_left], token=True,
    )
    exit_r = to_left(exit_r_left)
    *left_tables, done = call(
        table_kernel, "tables_left", [VMEM] * 4, [QUAD] * 4, [strip_a, dft, *settled_left[1:]],
        after=[done], token=True,
    )
    *own_tables, done = call(
        table_kernel, "tables", [VMEM] * 4, [QUAD] * 4, [strip_keep, dft, *settled[1:]],
        after=[done], token=True,
    )
    r_keep, r_send, done = terms(
        1, exit_l_left, exit_r_left, strip_b, *settled_left, *left_tables, psi1_left, w_left, after=[done], token=True
    )
    r_recv = to_other(r_send)
    l_keep, l_send = terms(0, exit_l, exit_r, record, *settled, *own_tables, psi1, w1, after=[done])
    l_recv = to_other(l_send)

    laid_out, laid = call(
        lay_out, "lay_out", [VMEM] * 5, [(transmission.shape, BF), ((2, height, W), BF)],
        [strip_keep, strip_a, l_keep, r_keep, r_recv], [pltpu.SemaphoreType.DMA((2,))], out_specs=[HBM, VMEM],
    )
    return call(
        finish, "finish", [VMEM] * 3 + [HBM], [(transmission.shape, BF)], [strip_keep, l_recv, laid, laid_out],
        [pltpu.VMEM((2, SPAN, W), BF), pltpu.SemaphoreType.DMA], out_specs=[HBM], aliases={3: 0},
    )[0]


def solution(mesh):
    in_specs = (
        P("depth", None, None, "tile"),
        P(),
        P(),
        P("tile", None, None, None),
        P("tile", None),
        P("tile", None),
        P("tile"),
    )
    out_specs = P("depth", None, None, "tile")
    return jax.shard_map(
        on_device, mesh=mesh, in_specs=in_specs, out_specs=out_specs, check_vma=False
    )
```

```python
import math

import jax
import jax.numpy as jnp
import numpy as np
from jax import lax
from jax.experimental import pallas as pl
from jax.experimental.pallas import tpu as pltpu
from jax.sharding import PartitionSpec as P

W = 256
STEP = 16
SPAN = W + STEP
LS = 16
RS = 4
EARLY = 48
EDGE = W - 8
BF = jnp.bfloat16
F32 = jnp.float32


def dot(a, b):
    return jnp.dot(a, b, preferred_element_type=F32)


def iota(shape, dim):
    return lax.broadcasted_iota(jnp.int32, shape, dim)


def dft_tables():
    indices = np.arange(W)
    angle = (indices[:, None] * indices[None, :] % W).astype(np.float64) * (2.0 * math.pi / W)
    factor = 1.0 / math.sqrt(W)
    cos = (np.cos(angle) * factor).astype(np.float32)
    sin = (np.sin(angle) * factor).astype(np.float32)
    return np.concatenate([cos, sin], axis=0)


def place(strip, slot):
    lane = iota((1, 128), 1)
    values = strip[W // 4 :].astype(F32)[0:1]
    row = jnp.sum(jnp.where(lane == slot * 4, values, jnp.where(lane == slot * 4 + 1, values * W, 0.0)))
    col = jnp.sum(jnp.where(lane == slot * 4 + 2, values, 0.0))
    return row.astype(jnp.int32), col.astype(jnp.int32)


def span(row, height):
    base = jnp.minimum(row & ~(STEP - 1), height - SPAN)
    return pl.multiple_of(base, STEP), row - base


def fold(buf, offset):
    lane = buf.shape[-1]
    top = jnp.where(iota((STEP, lane), 0) < offset, buf[W:SPAN].astype(F32), buf[0:STEP].astype(F32))
    return jnp.concatenate([top, buf[STEP:W].astype(F32)], axis=0)


def taps_table(taps, shift):
    a = (iota((W, 1), 0) - shift) & (W - 1)
    b = (iota((1, W), 1) - shift) & (W - 1)
    k = jnp.abs(a - b)
    out = jnp.zeros((W, W), F32)
    for distance in range(5):
        out = jnp.where(k == distance, taps[distance], out)
    return out.astype(BF)


def column_pass(re, im, t_col, sign):
    y = dot(jnp.concatenate([re.astype(BF), im.astype(BF)], axis=0), t_col)
    return re - sign * y[W:], im + sign * y[:W]


def propagate(re, im, t_row, t_col, sign):
    re, im = column_pass(re, im, t_col, sign)
    z = dot(t_row, jnp.concatenate([re.astype(BF), im.astype(BF)], axis=1))
    return re - sign * z[:, W:], im + sign * z[:, :W]


def one_hot(shift, transposed):
    if transposed:
        hit = iota((W, 1), 0) == ((iota((1, W), 1) - shift) & (W - 1))
    else:
        hit = iota((1, W), 1) == ((iota((W, 1), 0) - shift) & (W - 1))
    return jnp.where(hit, 1.0, 0.0).astype(BF)


def forward(w0, w1, psi0, t_row, t_col):
    p1 = propagate(w0[0] * psi0[0] - w0[1] * psi0[1], w0[0] * psi0[1] + w0[1] * psi0[0], t_row, t_col, 1.0)
    p1b = (p1[0].astype(BF), p1[1].astype(BF))
    q = (p1b[0].astype(F32), p1b[1].astype(F32))
    p2 = column_pass(w1[0] * q[0] - w1[1] * q[1], w1[0] * q[1] + w1[1] * q[0], t_col, 1.0)
    return p1b, (p2[0].astype(BF), p2[1].astype(BF))


def pack(parts, firsts, width):
    total = width * len(parts)
    blocks = 128 // total
    rows = W // blocks
    lane = iota((W, 128), 1)
    row = parts[0] if firsts[0] == 0 else pltpu.roll(parts[0], 128 - firsts[0], 1)
    for i in range(1, len(parts)):
        row = jnp.where(lane < i * width, row, pltpu.roll(parts[i], (i * width - firsts[i]) % 128, 1))
    out = row[:rows]
    for b in range(1, blocks):
        moved = pltpu.roll(row[b * rows : (b + 1) * rows], b * total, 1)
        out = jnp.where(lane[:rows] < b * total, out, moved)
    return out.astype(BF)


def unpack(packed, firsts, width):
    total = width * len(firsts)
    blocks = 128 // total
    values = packed.astype(F32)
    row = jnp.concatenate(
        [values] + [pltpu.roll(values, 128 - b * total, 1) for b in range(1, blocks)], axis=0
    )
    shifts = [(first - i * width) % 128 for i, first in enumerate(firsts)]
    return [pltpu.roll(row, shift, 1) if shift else row for shift in shifts]


def pair(own, other, mine):
    return jnp.where(mine == 0, own, other), jnp.where(mine == 0, other, own)


def windows_of(tile, other, mine, base, offset):
    rows = pl.ds(base, SPAN)
    out = []
    for i in range(2):
        for s, part in enumerate(pair(fold(tile[0, i, rows, :], offset), fold(other[0, i, rows, :], offset), mine)):
            out.append((s, i, part))
    return {(s, i): part for s, i, part in out}


def edges(
    pos_row, pos_col, chirp_taps, tile, records, strip_keep, strip_send,
    rows, cols, taps, record, side_buf, packed, packed_send, sems,
):
    mine = lax.axis_index("depth")
    height = tile.shape[2]
    pairs = [(pos_row, rows), (pos_col, cols), (chirp_taps, taps), (records.at[0, 1 - mine, EARLY:], record)]
    pairs += [(tile.at[0, i, :, pl.ds(W - 128, 128)], side_buf.at[i]) for i in range(2)]
    copies = [pltpu.make_async_copy(source, target, sems.at[k]) for k, (source, target) in enumerate(pairs)]
    for copy in copies:
        copy.start()
    last = []

    def put(source, target):
        last.append(pltpu.make_async_copy(source, target, sems.at[len(pairs) + len(last)]))
        last[-1].start()

    copies[0].wait()
    base, offset = span(rows[0, mine], height)
    base_send, offset_send = span(rows[0, 1 - mine], height)
    copies[1].wait()
    copies[2].wait()
    lane = iota((STEP, 128), 1)
    numbers = jnp.zeros((STEP, 128), jnp.int32)
    for slot in range(2):
        row, col = rows[0, slot], cols[0, slot]
        for k, part in enumerate((row & (W - 1), row >> 8, col)):
            numbers = jnp.where(lane == slot * 4 + k, part, numbers)
    numbers = numbers.astype(F32)
    for k in range(5):
        numbers = jnp.where(lane == 8 + k, taps[k], numbers)
    packed[W // 4 :] = numbers.astype(BF)
    copies[3].wait()
    put(record, strip_send.at[W // 8 :])
    copies[4].wait()
    copies[5].wait()
    strip = pack([fold(side_buf[i, pl.ds(base_send, SPAN), :], offset_send) for i in range(2)], [128 - LS] * 2, LS)
    packed_send[...] = jnp.concatenate([strip[: W // 8], strip[W // 8 :]], axis=1)
    put(packed_send, strip_send.at[: W // 8])
    packed[: W // 4] = pack([fold(side_buf[i, pl.ds(base, SPAN), :], offset) for i in range(2)], [128 - LS] * 2, LS)
    put(packed, strip_keep)
    for copy in last:
        copy.wait()


def settle(taps, probe, offset, col0, psi0, t_row, t_col):
    t_row[...], t_col[...] = taps_table(taps, offset), taps_table(taps, col0)
    for i in range(2):
        psi0[i] = pltpu.roll(pltpu.roll(probe[i], offset, 0), col0, 1)


def settle_own(pos_row, pos_col, chirp_taps, tile, probe, keep, psi0, t_row, t_col, rows, cols, taps, buf, sems):
    mine = lax.axis_index("depth")
    pairs = [(pos_row, rows), (pos_col, cols), (chirp_taps, taps)]
    copies = [pltpu.make_async_copy(source, target, sems.at[k]) for k, (source, target) in enumerate(pairs)]
    for copy in copies:
        copy.start()
    copies[0].wait()
    base, offset = span(rows[0, mine], tile.shape[2])
    whole = pltpu.make_async_copy(tile.at[0, :, pl.ds(base, SPAN), :], buf, sems.at[3])
    whole.start()
    copies[1].wait()
    copies[2].wait()
    settle(taps, probe, offset, cols[0, mine], psi0, t_row, t_col)
    whole.wait()
    for i in range(2):
        keep[i] = fold(buf[i], offset).astype(BF)


def settle_left(height, strip, probe, psi0, t_row, t_col):
    row, col0 = place(strip, lax.axis_index("depth"))
    _, offset = span(row, height)
    numbers = strip[W // 4 :].astype(F32)[0:1]
    settle([numbers[:, 8 + k : 9 + k] for k in range(5)], probe, offset, col0, psi0, t_row, t_col)


def tables(height, strip, dft, t_row, t_col, f_to, f_right, f_back, f_last):
    row, col0 = place(strip, lax.axis_index("depth"))
    _, offset = span(row, height)
    tall = dft[...]
    wide = jnp.concatenate([tall[:W], tall[W:]], axis=1)
    x = dot(tall, one_hot(offset, True)).astype(BF)
    y = dot(x, t_row[...])
    cos, sin = (x[:W].astype(F32) + y[W:]).astype(BF), (x[W:].astype(F32) - y[:W]).astype(BF)
    f_to[:W, :W], f_to[:W, W:], f_to[W:, :W], f_to[W:, W:] = cos, sin, -sin, cos
    x = dot(one_hot(col0, False), wide).astype(BF)
    cos, sin = x[:, :W], x[:, W:]
    f_right[:W, :W], f_right[:W, W:], f_right[W:, :W], f_right[W:, W:] = cos, -sin, sin, cos
    x = dot(one_hot(offset, False), wide).astype(BF)
    y = dot(t_row[...], x)
    cos, sin = (x[:, :W].astype(F32) + y[:, W:]).astype(BF), (x[:, W:].astype(F32) - y[:, :W]).astype(BF)
    f_back[:W, :W], f_back[:W, W:], f_back[W:, :W], f_back[W:, W:] = cos, -sin, sin, cos
    x = dot(tall, one_hot(col0, True)).astype(BF)
    y = dot(x, t_col[...])
    cos, sin = (x[:W].astype(F32) + y[W:]).astype(BF), (x[W:].astype(F32) - y[:W]).astype(BF)
    f_last[:W, :W], f_last[:W, W:], f_last[W:, :W], f_last[W:, W:] = cos, sin, -sin, cos


def put_exit(exit_ref, psi2, inside):
    for i in range(2):
        part = jnp.where(inside, psi2[i], 0.0).astype(BF)
        for half in range(2):
            exit_ref[(2 * i + half) * W : (2 * i + half + 1) * W] = part[:, half * 128 : (half + 1) * 128]


def left_forward(strip, live, record, keep, other, psi0, t_row, t_col, exit_ref, w_ref, psi1_ref):
    mine = lax.axis_index("depth")
    row, col0 = place(strip, mine)
    base, offset = span(row, other.shape[2])
    column = iota((1, W), 1)
    inside = column >= col0
    w = {}
    for i in range(2):
        far = fold(other[0, i, pl.ds(base, SPAN), :], offset)
        for s, part in enumerate(pair(keep[i].astype(F32), far, mine)):
            w[s, i] = jnp.where(inside, part, 0.0)
    w_ref[0], w_ref[1] = w[1, 0].astype(BF), w[1, 1].astype(BF)
    psi1, psi2 = forward((w[0, 0], w[0, 1]), (w[1, 0], w[1, 1]), psi0, t_row[...], t_col[...])
    psi1_ref[0], psi1_ref[1] = psi1
    put_exit(exit_ref, psi2, inside & (column < EDGE))
    number, lane = iota((STEP, 128), 0), iota((STEP, 128), 1)
    marks = jnp.where(lane + jnp.where(number == 2, 128, 0) >= col0, 1.0, 0.0)
    exit_ref[4 * W : 4 * W + STEP] = jnp.where(number == 0, live[...], marks).astype(BF)
    for half in range(2):
        start = 4 * W + STEP + half * EARLY
        exit_ref[start : start + EARLY] = record[:EARLY, half * 128 : (half + 1) * 128]


def right_forward(
    tile, other, strip_a, strip_b, psi0, t_row, t_col, exit_ref, w_ref, psi1_ref
):
    mine = lax.axis_index("depth")
    row, col0 = place(strip_a, mine)
    base, offset = span(row, tile.shape[2])
    lane, column = iota((1, 128), 1), iota((1, W), 1)
    across = strip_b[: W // 8]
    across = jnp.concatenate([across[:, :128], across[:, 128:]], axis=0)
    strips = pair(strip_a[: W // 4].astype(F32), across.astype(F32), mine)
    w = windows_of(tile, other, mine, base, offset)
    for s in range(2):
        lefts = unpack(strips[s], [128 - LS] * 2, LS)
        for i in range(2):
            left = jnp.where(lane >= 128 - LS, lefts[i], 0.0)
            low = jnp.where(lane < col0, w[s, i][:, :128], 0.0)
            high = jnp.where(lane + 128 < col0, w[s, i][:, 128:], left)
            w[s, i] = jnp.concatenate([low, high], axis=1)
    w_ref[0], w_ref[1] = w[1, 0].astype(BF), w[1, 1].astype(BF)
    psi1, psi2 = forward((w[0, 0], w[0, 1]), (w[1, 0], w[1, 1]), psi0, t_row[...], t_col[...])
    psi1_ref[0], psi1_ref[1] = psi1
    put_exit(exit_ref, psi2, (column < col0) | (column >= EDGE))
    parts = [psi1[0][:, 128:].astype(F32), psi1[1][:, 128:].astype(F32), w[1, 0][:, :128], w[1, 1][:, :128]]
    exit_ref[4 * W :] = pack(parts, [128 - RS, 128 - RS, 0, 0], RS)


def far_field(
    side, exit_l, exit_r, record, psi0, t_row, t_col, f_to, f_right, f_back, f_last, psi1, w1, keep, send
):
    mine = lax.axis_index("depth")
    notes = exit_l[4 * W : 4 * W + STEP].astype(F32)
    live = notes[0:1, 0:1]
    of_left = jnp.concatenate([notes[1:2], notes[2:3]], axis=1)
    region = of_left if side == 0 else 1.0 - of_left
    lane = iota((1, 128), 1)
    halves = [exit_l[k * W : (k + 1) * W] + exit_r[k * W : (k + 1) * W] for k in range(4)]
    wave = jnp.concatenate([jnp.concatenate(halves[:2], axis=1), jnp.concatenate(halves[2:], axis=1)], axis=0)
    x = dot(f_to[...], wave).astype(BF)
    x = dot(jnp.concatenate([x[:W], x[W:]], axis=1), f_right[...])
    fr, fi = x[:, :W], x[:, W:]
    if side == 1:
        early = exit_l[4 * W + STEP :]
        early = jnp.concatenate([early[:EARLY], early[EARLY:]], axis=1)
        record = jnp.concatenate([early, record[W // 8 :]], axis=0)
    misfit = (fr * fr + fi * fi - record[...].astype(F32)) * live
    x = dot(f_back[...], jnp.concatenate([(misfit * fr).astype(BF), (misfit * fi).astype(BF)], axis=0)).astype(BF)
    x = dot(jnp.concatenate([x[:W], x[W:]], axis=1), f_last[...])
    q1 = x[:, :W], x[:, W:]
    psi = [psi1[i].astype(F32) for i in range(2)]
    w = [w1[i].astype(F32) for i in range(2)]
    if side == 0:
        strips = unpack(exit_r[4 * W :], [128 - RS, 128 - RS, 0, 0], RS)
        for i in range(2):
            high = jnp.where(lane >= 128 - RS, strips[i], psi[i][:, 128:])
            psi[i] = jnp.concatenate([psi[i][:, :128], high], axis=1)
            low = jnp.where(lane < RS, w[i][:, :128] + strips[2 + i] * (1.0 - of_left[:, :128]), w[i][:, :128])
            w[i] = jnp.concatenate([low, w[i][:, 128:]], axis=1)

    def term(psi_r, psi_i, q):
        return (psi_r * q[0] + psi_i * q[1]) * region, (psi_r * q[1] - psi_i * q[0]) * region

    term1 = term(psi[0], psi[1], q1)
    cr = (w[0] * q1[0] + w[1] * q1[1]).astype(BF).astype(F32)
    ci = (w[0] * q1[1] - w[1] * q1[0]).astype(BF).astype(F32)
    q0 = propagate(cr, ci, t_row[...], t_col[...], -1.0)
    term0 = term(psi0[0], psi0[1], q0)
    for i in range(2):
        first, second = pair(term0[i], term1[i], mine)
        keep[i], send[i] = first.astype(BF), second.astype(BF)


def add_part(buf, i, base, offset, term):
    mask = iota((STEP, 1), 0) >= offset
    top = term[i, 0:STEP].astype(F32)
    rows = pl.ds(base, STEP)
    buf[i, rows, :] = buf[i, rows, :] + jnp.where(mask, top, 0.0).astype(BF)
    rows = pl.ds(base + STEP, W - STEP) if isinstance(base, int) else pl.ds(pl.multiple_of(base + STEP, STEP), W - STEP)
    buf[i, rows, :] = buf[i, rows, :] + term[i, STEP:W]
    rows = pl.ds(base + W, STEP) if isinstance(base, int) else pl.ds(pl.multiple_of(base + W, STEP), STEP)
    buf[i, rows, :] = buf[i, rows, :] + jnp.where(mask, 0.0, top).astype(BF)


def lay_out(own, left, l_keep, r_keep, r_recv, out, buf, sems):
    height = out.shape[2]
    mine = lax.axis_index("depth")
    work = []
    for where, slot, term in ((left, mine, r_keep), (left, 1 - mine, r_recv), (own, mine, l_keep)):
        row, _ = place(where, slot)
        base, offset = span(row, height)
        work.append((base, offset, term))
    copies = []
    for i in range(2):
        buf[i] = jnp.zeros((height, W), BF)
        for base, offset, term in work:
            add_part(buf, i, base, offset, term)
        copy = pltpu.make_async_copy(buf.at[i], out.at[0, i], sems.at[i])
        copy.start()
        copies.append(copy)
    for copy in copies:
        copy.wait()


def finish(own, l_recv, laid, before, out, buf, sem):
    del before
    row, _ = place(own, 1 - lax.axis_index("depth"))
    base, offset = span(row, out.shape[2])
    rows = pl.ds(base, SPAN)
    for i in range(2):
        buf[i] = laid[i, rows, :]
        add_part(buf, i, 0, offset, l_recv)
    copy = pltpu.make_async_copy(buf, out.at[0, :, rows, :], sem)
    copy.start()
    copy.wait()


VMEM = pl.BlockSpec(memory_space=pltpu.VMEM)
HBM = pl.BlockSpec(memory_space=pltpu.HBM)


def call(kernel, name, specs, outs, args, scratch=(), out_specs=None, vmem=40, after=(), token=False, aliases=None):
    count, extra, made = len(args), len(after), len(outs)

    def body(*refs):
        refs = list(refs)
        if token:
            refs.pop(count + extra + made)[...] = jnp.zeros((8, 128), F32)
        kernel(*refs[:count], *refs[count + extra :])

    outs, out_specs = list(outs), list(out_specs or [VMEM] * made)
    if token:
        outs, out_specs = outs + [((8, 128), F32)], out_specs + [VMEM]
    moved = sum(math.prod(shape) * jnp.dtype(kind).itemsize for shape, kind in outs)
    moved += sum(math.prod(a.shape) * a.dtype.itemsize for a, s in zip(args, specs) if s is not HBM)
    return pl.pallas_call(
        body,
        name=name,
        out_shape=[jax.ShapeDtypeStruct(shape, kind) for shape, kind in outs],
        in_specs=list(specs) + [VMEM] * extra,
        out_specs=out_specs,
        scratch_shapes=list(scratch),
        input_output_aliases=aliases or {},
        compiler_params=pltpu.CompilerParams(vmem_limit_bytes=vmem * 1024 * 1024),
        cost_estimate=pl.CostEstimate(flops=10**9, bytes_accessed=moved, transcendentals=0),
    )(*args, *after)


FIELD, WAVE = ((2, W, W), BF), ((2, W, W), F32)
BAND, QUAD = ((W, W), BF), ((2 * W, 2 * W), BF)
MARKED, LOADED = ((W // 4 + STEP, 128), BF), ((W // 8 + W - EARLY, W), BF)
EXIT_L, EXIT_R = ((4 * W + STEP + 2 * EARLY, 128), BF), ((4 * W + W * 4 * RS // 128, 128), BF)


def on_device(transmission, chirp_taps, probe_field, records, pos_row, pos_col, counts):
    height = transmission.shape[2]
    tiles = lax.axis_size("tile")
    my_depth = lax.axis_index("depth")

    def to_right(x):
        return lax.ppermute(x, "tile", [(i, (i + 1) % tiles) for i in range(tiles)])

    def to_left(x):
        return lax.ppermute(x, "tile", [(i, (i - 1) % tiles) for i in range(tiles)])

    def to_right_other(x):
        pairs = [(d * tiles + i, (1 - d) * tiles + (i + 1) % tiles) for d in range(2) for i in range(tiles)]
        return lax.ppermute(x, ("depth", "tile"), pairs)

    def to_other(x):
        return lax.ppermute(x, "depth", [(0, 1), (1, 0)])

    def table_kernel(*refs):
        tables(height, *refs)

    def settle_left_kernel(*refs):
        settle_left(height, *refs)

    def terms(side, *args, after=(), token=False):
        def kernel(*refs):
            far_field(side, *refs)

        return call(
            kernel, f"far_field_{side}", [VMEM] * len(args), [FIELD, FIELD], args, after=after, token=token
        )

    dft = jnp.asarray(dft_tables(), BF)
    other_tile = to_other(transmission)
    record = lax.dynamic_index_in_dim(records[0], my_depth, 0, keepdims=False)
    scalars = [pltpu.SMEM((1, 2), jnp.int32)] * 2 + [pltpu.SMEM((5,), F32)]
    shapes = (W - EARLY, W), (2, height, 128), MARKED[0], (W // 8, W)
    strip_keep, strip_send = call(
        edges, "edges", [HBM] * 5, [MARKED, LOADED], [pos_row, pos_col, chirp_taps, transmission, records],
        scalars + [pltpu.VMEM(shape, BF) for shape in shapes] + [pltpu.SemaphoreType.DMA((9,))],
        out_specs=[HBM] * 2, vmem=56,
    )
    strip_a = to_right(strip_keep)
    strip_b = to_right_other(strip_send)
    live = jnp.broadcast_to((my_depth < counts[0]).astype(F32), (STEP, 128))
    keep, *settled = call(
        settle_own, "settle", [HBM] * 4 + [VMEM], [FIELD, WAVE, BAND, BAND],
        [pos_row, pos_col, chirp_taps, transmission, probe_field],
        scalars + [pltpu.VMEM((2, SPAN, W), BF), pltpu.SemaphoreType.DMA((4,))], vmem=51,
    )
    exit_l, w1, psi1, done = call(
        left_forward, "left_forward", [VMEM] * 8, [EXIT_L, FIELD, FIELD],
        [strip_keep, live, record, keep, other_tile, *settled], token=True,
    )
    exit_l_left = to_right(exit_l)
    settled_left = call(
        settle_left_kernel, "settle_left", [VMEM] * 2, [WAVE, BAND, BAND], [strip_a, probe_field], after=[done]
    )
    exit_r_left, w_left, psi1_left, done = call(
        right_forward, "right_forward", [VMEM] * 7, [EXIT_R, FIELD, FIELD],
        [transmission, other_tile, strip_a, strip_b, *settled_left], token=True,
    )
    exit_r = to_left(exit_r_left)
    *left_tables, done = call(
        table_kernel, "tables_left", [VMEM] * 4, [QUAD] * 4, [strip_a, dft, *settled_left[1:]],
        after=[done], token=True,
    )
    *own_tables, done = call(
        table_kernel, "tables", [VMEM] * 4, [QUAD] * 4, [strip_keep, dft, *settled[1:]],
        after=[done], token=True,
    )
    r_keep, r_send, done = terms(
        1, exit_l_left, exit_r_left, strip_b, *settled_left, *left_tables, psi1_left, w_left, after=[done], token=True
    )
    r_recv = to_other(r_send)
    l_keep, l_send = terms(0, exit_l, exit_r, record, *settled, *own_tables, psi1, w1, after=[done])
    l_recv = to_other(l_send)

    laid_out, laid = call(
        lay_out, "lay_out", [VMEM] * 5, [(transmission.shape, BF), ((2, height, W), BF)],
        [strip_keep, strip_a, l_keep, r_keep, r_recv], [pltpu.SemaphoreType.DMA((2,))], out_specs=[HBM, VMEM],
    )
    return call(
        finish, "finish", [VMEM] * 3 + [HBM], [(transmission.shape, BF)], [strip_keep, l_recv, laid, laid_out],
        [pltpu.VMEM((2, SPAN, W), BF), pltpu.SemaphoreType.DMA], out_specs=[HBM], aliases={3: 0},
    )[0]


def solution(mesh):
    in_specs = (
        P("depth", None, None, "tile"),
        P(),
        P(),
        P("tile", None, None, None),
        P("tile", None),
        P("tile", None),
        P("tile"),
    )
    out_specs = P("depth", None, None, "tile")
    return jax.shard_map(
        on_device, mesh=mesh, in_specs=in_specs, out_specs=out_specs, check_vma=False
    )
```
